32 devices in a mesh: dp: 16 (over z, y, x), feat: 2 (over core).
Axes of the slice: x: 2, y: 2, z: 4, core: 2. Of those that a mesh axis runs over, the one named last changes fastest.
Arguments:
- grads: bfloat16 [2, 8192, 4, 128], P('feat', 'dp'), may hold values from -6 to 6
- block_ids: int32 [2, 8192, 4], P('feat', 'dp'), may hold values from 0 to 511, all different within a row; in each aligned block of 512 rows (0 to 511, 512 to 1023, ..., all dimensions but the last counted through in order) at most 6 rows name the same one
- probe: bfloat16 [512, 2, 128, 512], P('dp', 'feat'), may hold values from -0.1875 to 0.1875
Outputs:
- whitened: float32 [8192, 512], P(('dp', 'feat'))
The draws below stay inside these ranges and needn't reach their ends.
Inputs may be any that keep to these rules, and one draw needn't show every extreme that they name: block_ids[j, s, k] is a local block number in slice j; the ids of one sample in one slice are distinct; among the 512 samples of one index of dp, no number appears more than 6 times in one slice, and some number appears exactly 6 times.
All inputs are finite; a program needn't handle non-finite values.
Results may differ from the reference program's by a relative error of at most 0.012.
Values may be sent and summed in bfloat16 or wider, within the bound.
No kernel may reach another device: no remote copies, remote signals or barrier semaphores. Data moves between devices by JAX's collectives and lax.ppermute only.
A program may use at most 128 MiB of HBM per device.

```python
import math
import jax
import jax.numpy as jnp
import numpy as np
from jax import lax

BW = 128
RANK = 512
K_J = 4
S_DEV = 512
SLICES = 2
SAMPLES = 8192
BF = 512
MOST = 6
KTOT = 8


def steps_of(own_key, extent, shards, smallest, largest):
    level, own = 1.0, jax.random.fold_in(own_key, 6)
    for axis_at, parts in shards:
        draws = jnp.exp(jax.random.uniform(jax.random.fold_in(own, axis_at), (parts,), jnp.float32, smallest / len(shards), largest / len(shards)))
        level = level * jnp.repeat(draws, extent[axis_at] // parts).reshape([-1 if axis == axis_at else 1 for axis in range(len(extent))])
    return level


def assign_block(own_key, own, number, rows, count, top, most, lean):
    ranking = jax.random.permutation(own_key, count)
    heavy_load, ordinary = portions_of(count, rows * top, most, lean, True), portions_of(count, rows * top, most, lean, False)
    places = jnp.arange(count)

    def named(tallies, turn):
        used = int((tallies > 0).sum())
        fixed = max(1, used // 4)
        moved = fixed + (places - fixed + turn * (used - fixed)) % max(1, count - fixed)
        return jnp.zeros((count,), jnp.int32).at[ranking[jnp.where(places < fixed, places, moved)]].set(jnp.asarray(tallies, jnp.int32))

    tallies = jnp.where(number % 4 == 0, named(heavy_load, number // 4), named(ordinary, number - number // 4 - 1))
    mixed = jax.random.permutation(jax.random.fold_in(own, 3), count)
    source_of, sink = mixed[0:count // 2 * 2:2], mixed[1:count // 2 * 2:2]
    slack = jnp.minimum(tallies[source_of] - 1, most - tallies[sink]) // 2
    slack = jnp.where((source_of == ranking[0]) | (sink == ranking[0]) | (tallies[sink] == 0), 0, jnp.maximum(slack, 0))
    moved = jax.random.randint(jax.random.fold_in(own, 4), (count // 2,), 0, 1 << 20) % (slack + 1)
    tallies = tallies.at[source_of].add(-moved).at[sink].add(moved)
    labels = jnp.searchsorted(jnp.cumsum(tallies), jnp.arange(rows * top), side="right").astype(jnp.int32)
    grid = labels.reshape(top, rows).T
    grid = grid[jax.random.permutation(jax.random.fold_in(own, 1), rows)]
    turn = jax.random.randint(jax.random.fold_in(own, 2), (rows, 1), 0, top)
    return jnp.take_along_axis(grid, (jnp.arange(top)[None, :] + turn) % top, axis=1)


def portions_of(count, total, most, skew, full):
    weights = [(1 << 20) // math.isqrt(grade ** skew) + 1 for grade in range(1, count + 1)]
    largest = most if full else min(most, max(-(-total // count), total * weights[0] // sum(weights)))
    least = 1 if total - largest >= count - 1 else 0
    given, spare = [largest] + [least] * (count - 1), total - largest - least * (count - 1)
    while spare > 0:
        movable = [i for i in range(1, count) if given[i] < largest] or [i for i in range(1, count) if given[i] < most]
        whole, left = sum([weights[i] for i in movable]), spare
        for i in movable:
            extra = min(most - given[i], max(1, left * weights[i] // whole), spare)
            given[i] = given[i] + extra
            spare = spare - extra
    return np.array(given)


def gaussian(key, shape, deviation, bound, cuts=(), kind=jnp.bfloat16):
    values = deviation * jax.random.normal(key, shape, jnp.float32)
    if cuts:
        values = values * steps_of(key, shape, cuts, -0.22, 0.18)
    return jnp.clip(values, -bound, bound).astype(kind)


def setup_inputs(seed: int = 0) -> dict:
    arg_keys = jax.random.split(jax.random.key(seed), 4)
    grads = gaussian(arg_keys[0], (SLICES, SAMPLES, K_J, BW), 1.0, 6.0, ((0, 2), (1, 16)))
    block_ids_keys = jax.random.split(jax.random.fold_in(arg_keys[1], 1), SLICES * SAMPLES // S_DEV)
    block_ids_turns = jax.random.permutation(jax.random.fold_in(arg_keys[1], 3), SLICES * SAMPLES // S_DEV)
    block_ids = jax.vmap(lambda own, number: assign_block(jax.random.fold_in(arg_keys[1], 2), own, number, S_DEV, BF, K_J, MOST, 2))(block_ids_keys, block_ids_turns).reshape((SLICES, SAMPLES, K_J))
    probe = gaussian(arg_keys[2], (BF, SLICES, BW, RANK), (KTOT * BW) ** -0.5, 0.1875, ((0, 16), (1, 2)))
    return {"grads": grads, "block_ids": block_ids, "probe": probe}


root_steps = 4

def inverse_root(gram):
    width = gram.shape[0]
    ident = jnp.eye(width, dtype=jnp.float32)
    scale = jnp.trace(gram) / width
    current = gram / scale
    result = ident
    for step in range(root_steps):
        middle = 1.5 * ident - 0.5 * jnp.dot(result, current, precision=lax.Precision.HIGHEST)
        if step + 1 < root_steps:
            current = jnp.dot(current, middle, precision=lax.Precision.HIGHEST)
        result = jnp.dot(middle, result, precision=lax.Precision.HIGHEST)
    return result / jnp.sqrt(scale)

def reference(grads, block_ids, probe):
    slices = grads.shape[0]
    samples = grads.shape[1]
    group = 8
    g_blocks = grads.reshape(slices, samples // group, group, K_J, BW).transpose(1, 0, 2, 3, 4)
    i_blocks = block_ids.reshape(slices, samples // group, group, K_J).transpose(1, 0, 2, 3)
    slice_index = jnp.arange(slices, dtype=jnp.int32)[:, None, None]

    def one_group(pair):
        values, ids = pair
        rows = probe[ids, slice_index]
        prod = jnp.einsum('jskb,jskbr->jskr', values.astype(jnp.float32), rows.astype(jnp.float32))
        prod = prod.astype(jnp.bfloat16)
        return lax.optimization_barrier(jnp.sum(prod.astype(jnp.float32), axis=(0, 2)))
    sketch_sum = lax.map(one_group, (g_blocks, i_blocks)).reshape(samples, RANK)
    sketch = sketch_sum.astype(jnp.bfloat16)
    gram = lax.dot_general(sketch, sketch, (((0,), (0,)), ((), ())), preferred_element_type=jnp.float32)
    gram = gram + 0.1 * samples * jnp.eye(RANK, dtype=jnp.float32)
    root = inverse_root(gram)
    return math.sqrt(samples) * jnp.dot(sketch.astype(jnp.float32), root, precision=lax.Precision.HIGHEST)
```

```python
import functools
import math

import jax
import jax.numpy as jnp
import numpy as np
from jax import lax
from jax.experimental import pallas as pl
from jax.experimental.pallas import tpu as pltpu
from jax.sharding import PartitionSpec as P

ridge = 0.1
root_steps = 4
f32 = jnp.float32
bf16 = jnp.bfloat16
lane = 128
vmem_limit = 48 << 20

COLS = (((0,), (0,)), ((), ()))


def params(**kw):
    return pltpu.CompilerParams(vmem_limit_bytes=vmem_limit, **kw)


def whole():
    return pl.BlockSpec(memory_space=pltpu.VMEM)


def pack_kernel(per_dev, bound, direct, ids_ref, values_ref, send_ref, position_ref):
    k_j, s_dev = ids_ref.shape
    n_ids = send_ref.shape[0] * per_dev if direct else send_ref.shape[1]
    width = lane
    ids_rows = ids_ref[...]
    padded = jnp.concatenate([ids_rows.astype(f32), jnp.zeros((lane - k_j, s_dev), f32)], axis=0)
    ids_cols = jnp.transpose(padded)
    numbers = lax.broadcasted_iota(jnp.int32, (s_dev, n_ids), 1).astype(f32)
    number_rows = lax.broadcasted_iota(jnp.int32, (n_ids, s_dev), 0)
    earlier = (
        lax.broadcasted_iota(jnp.int32, (s_dev, s_dev), 0) > lax.broadcasted_iota(jnp.int32, (s_dev, s_dev), 1)
    )
    earlier = jnp.where(earlier, 1.0, 0.0).astype(bf16)
    used = jnp.zeros((1, n_ids), f32)
    total = jnp.zeros((n_ids, bound * width), f32)
    places = []
    for k in range(k_j):
        column = ids_cols[:, k : k + 1]
        named = jnp.where(column == numbers, 1.0, 0.0)
        before = jnp.dot(earlier, named.astype(bf16), preferred_element_type=f32) + used
        rank = jnp.sum(named * before, axis=1, keepdims=True)
        used = used + jnp.sum(named, axis=0, keepdims=True)
        tile = values_ref[:, k * width : (k + 1) * width].astype(f32)
        by_rank = jnp.concatenate([jnp.where(rank == r, tile, 0.0).astype(bf16) for r in range(bound)], axis=1)
        named_rows = jnp.where(ids_rows[k : k + 1, :] == number_rows, 1.0, 0.0).astype(bf16)
        total = total + jnp.dot(named_rows, by_rank, preferred_element_type=f32)
        id_col = column.astype(jnp.int32)
        target = id_col // per_dev
        within = id_col - target * per_dev
        places.append((target * bound + rank.astype(jnp.int32)) * per_dev + within)
    position_ref[...] = jnp.concatenate(places, axis=1)
    for r in range(bound):
        rows = total[:, r * width : (r + 1) * width].astype(bf16)
        if direct:
            send_ref[:, r * per_dev : (r + 1) * per_dev, :] = rows.reshape(n_ids // per_dev, per_dev, width)
        else:
            send_ref[r] = rows


def pack(ids, values, n_dp, per_dev, bound):
    k_j, s_dev = ids.shape
    direct = per_dev % 16 == 0
    shape = (n_dp, bound * per_dev, lane) if direct else (bound, n_dp * per_dev, lane)
    send, position = pl.pallas_call(
        functools.partial(pack_kernel, per_dev, bound, direct),
        out_shape=(
            jax.ShapeDtypeStruct(shape, bf16),
            jax.ShapeDtypeStruct((s_dev, k_j), jnp.int32),
        ),
        in_specs=[whole(), whole()],
        out_specs=(whole(), whole()),
        compiler_params=params(),
        name="pack",
    )(ids, values)
    if not direct:
        send = send.reshape(bound, n_dp, per_dev, lane).transpose(1, 0, 2, 3).reshape(n_dp, bound * per_dev, lane)
    return send, position


def product_kernel(per_dev, per_step, tiles_ref, probe_ref, out_ref, tiles, products):
    step = pl.program_id(0)
    count = tiles.shape[0] // per_dev

    @pl.when(step == 0)
    def _():
        tiles[...] = tiles_ref[...].astype(f32)

    for at in range(per_step):
        block = step * per_step + at
        rows = pl.ds(block, count, stride=per_dev)
        value = jnp.dot(tiles[rows, :].astype(bf16), probe_ref[at], preferred_element_type=f32)
        for c in range(products.shape[0]):
            products[c, rows, :] = value[:, c * lane : (c + 1) * lane]

    @pl.when(step == pl.num_programs(0) - 1)
    def _():
        for c in range(products.shape[0]):
            out_ref[:, c * lane : (c + 1) * lane] = products[c].astype(bf16)


def product(tiles, probe):
    rows = tiles.shape[0]
    per_dev, _, width = probe.shape
    per_step = math.gcd(per_dev, 4)
    return pl.pallas_call(
        functools.partial(product_kernel, per_dev, per_step),
        out_shape=jax.ShapeDtypeStruct((rows, width), bf16),
        grid=(per_dev // per_step,),
        in_specs=[
            pl.BlockSpec((rows, lane), lambda i: (0, 0)),
            pl.BlockSpec((per_step, lane, width), lambda i: (i, 0, 0)),
        ],
        out_specs=pl.BlockSpec((rows, width), lambda i: (0, 0)),
        scratch_shapes=[pltpu.VMEM((rows, lane), f32), pltpu.VMEM((width // lane, rows, lane), f32)],
        compiler_params=params(),
        name="product",
    )(tiles, probe)


def combine_kernel(position_ref, rows_ref, out_ref):
    step = pl.program_id(0)
    s_dev, k_j = position_ref.shape
    count = rows_ref.shape[0]
    here = lax.broadcasted_iota(jnp.int32, (s_dev, count), 1) + step * count
    position = position_ref[...]
    hit = position[:, 0:1] == here
    for k in range(1, k_j):
        hit = jnp.logical_or(hit, position[:, k : k + 1] == here)
    part = jnp.dot(jnp.where(hit, 1.0, 0.0).astype(bf16), rows_ref[...], preferred_element_type=f32)

    @pl.when(step == 0)
    def _():
        out_ref[...] = part

    @pl.when(step > 0)
    def _():
        out_ref[...] += part


def combine(position, rows):
    s_dev, k_j = position.shape
    total, width = rows.shape
    count = total // 6 if total % (6 * lane) == 0 else total
    return pl.pallas_call(
        combine_kernel,
        out_shape=jax.ShapeDtypeStruct((s_dev, width), f32),
        grid=(total // count,),
        in_specs=[
            pl.BlockSpec((s_dev, k_j), lambda i: (0, 0)),
            pl.BlockSpec((count, width), lambda i: (i, 0)),
        ],
        out_specs=pl.BlockSpec((s_dev, width), lambda i: (0, 0)),
        compiler_params=params(),
        name="combine",
    )(position, rows)


def block_pairs(width):
    n = width // lane
    return [(i, j) for i in range(n) for j in range(i, n)]


def gram_kernel(own_rows, pairs_ref, place_ref, sum_a_ref, sum_b_ref, gram_ref, mine_ref, sketch):
    sketch[...] = (sum_a_ref[...] + sum_b_ref[...]).astype(bf16)
    start = pl.multiple_of(place_ref[0] * own_rows, own_rows)
    mine_ref[...] = sketch[pl.ds(start, own_rows), :]
    for at in range(gram_ref.shape[0]):
        left = sketch[:, pl.ds(pl.multiple_of(pairs_ref[2 * at] * lane, lane), lane)]
        right = sketch[:, pl.ds(pl.multiple_of(pairs_ref[2 * at + 1] * lane, lane), lane)]
        gram_ref[at] = lax.dot_general(left, right, COLS, preferred_element_type=f32)


def gram_blocks(sum_a, sum_b, place, n_feat):
    s_dev, width = sum_a.shape
    pairs = block_pairs(width)
    half = len(pairs) // 2
    table = jnp.asarray(np.array(pairs, np.int32).reshape(2, 2 * half))
    own_rows = s_dev // n_feat
    smem = pl.BlockSpec(memory_space=pltpu.SMEM)
    return pl.pallas_call(
        functools.partial(gram_kernel, own_rows),
        out_shape=(
            jax.ShapeDtypeStruct((half, lane, lane), f32),
            jax.ShapeDtypeStruct((own_rows, width), bf16),
        ),
        in_specs=[smem, smem, whole(), whole()],
        out_specs=(whole(), whole()),
        scratch_shapes=[pltpu.VMEM((s_dev, width), bf16)],
        compiler_params=params(),
        name="gram",
    )(table[place % 2], place.reshape(1), sum_a, sum_b)


def halves(value):
    high = value.astype(bf16)
    return high, (value - high.astype(f32)).astype(bf16)


def dot3(a, b):
    (ah, al), (bh, bl) = a, b
    out = jnp.dot(ah, bl, preferred_element_type=f32)
    if al is not None:
        out = out + jnp.dot(al, bh, preferred_element_type=f32)
    return out + jnp.dot(ah, bh, preferred_element_type=f32)


def root_kernel(samples, place_ref, mine_gram_ref, other_gram_ref, mine_ref, out_ref, gram):
    width = mine_ref.shape[1]
    pairs = block_pairs(width)
    half = len(pairs) // 2
    odd = place_ref[0] % 2 == 1
    for at, (i, j) in enumerate(pairs):
        mine, other = mine_gram_ref[at % half], other_gram_ref[at % half]
        block = jnp.where(odd, other, mine) if at < half else jnp.where(odd, mine, other)
        gram[i * lane : (i + 1) * lane, j * lane : (j + 1) * lane] = block
        if i != j:
            gram[j * lane : (j + 1) * lane, i * lane : (i + 1) * lane] = jnp.transpose(block)
    rows = lax.broadcasted_iota(jnp.int32, (width, width), 0)
    ident = jnp.where(rows == lax.broadcasted_iota(jnp.int32, (width, width), 1), 1.0, 0.0)
    total = gram[...] + ridge * samples * ident
    scale = jnp.sum(total * ident, axis=(0, 1), keepdims=True) / width
    current = total / scale
    result = (mine_ref[...], None)
    for step in range(root_steps):
        middle = halves(1.5 * ident - 0.5 * current)
        if step + 1 < root_steps:
            current = dot3(halves(dot3(halves(current), middle)), middle)
        value = dot3(result, middle)
        result = halves(value)
    out_ref[...] = (math.sqrt(samples) * lax.rsqrt(scale)) * value


def whiten(mine_gram, other_gram, mine, place, samples):
    width = mine.shape[1]
    return pl.pallas_call(
        functools.partial(root_kernel, samples),
        out_shape=jax.ShapeDtypeStruct(mine.shape, f32),
        in_specs=[pl.BlockSpec(memory_space=pltpu.SMEM), whole(), whole(), whole()],
        out_specs=whole(),
        scratch_shapes=[pltpu.VMEM((width, width), f32)],
        compiler_params=params(),
        name="root",
    )(place.reshape(1), mine_gram, other_gram, mine)


def crossed(value, axis, bits):
    count = lax.axis_size(axis)
    return lax.ppermute(value, axis, [(source, source ^ bits) for source in range(count)])


def sum_over_dp(value):
    n_dp = lax.axis_size("dp")
    index = lax.axis_index("dp")
    inner = math.gcd(n_dp, 4)
    flat = value.reshape(-1, lane)
    rows = flat.shape[0] // inner
    me = index % inner
    part = lax.dynamic_slice_in_dim(flat, me * rows, rows, 0)
    arrived = [
        crossed(lax.dynamic_slice_in_dim(flat, (me ^ bits) * rows, rows, 0), "dp", bits) for bits in range(1, inner)
    ]
    for other in arrived:
        part = part + other
    if n_dp // inner == 4:
        arrived = [crossed(part, "dp", bits * inner) for bits in range(1, 4)]
        for other in arrived:
            part = part + other
    else:
        bits = inner
        while bits < n_dp:
            part = part + crossed(part, "dp", bits)
            bits *= 2
    pieces = [part] + [crossed(part, "dp", bits) for bits in range(1, inner)]
    stacked = jnp.stack(pieces)
    ordered = [stacked[me ^ at] for at in range(inner)]
    return jnp.concatenate(ordered, axis=0).reshape(value.shape)


def local(grads, block_ids, probe):
    values = grads[0]
    s_dev, k_j, b_width = values.shape
    n_dp = lax.axis_size("dp")
    n_feat = lax.axis_size("feat")
    per_dev = probe.shape[0]
    width = probe.shape[3]
    b_slice = per_dev * n_dp
    bound = max(2, 3 * s_dev * k_j // (2 * b_slice))
    place = lax.axis_index("feat")
    send, position = pack(block_ids[0].T, values.reshape(s_dev, k_j * b_width), n_dp, per_dev, bound)
    tiles = lax.all_to_all(send, "dp", split_axis=0, concat_axis=0, tiled=True)
    products = product(tiles.reshape(-1, b_width), probe[:, 0])
    returned = lax.all_to_all(
        products.reshape(n_dp, -1, width), "dp", split_axis=0, concat_axis=0, tiled=True
    )
    part = combine(position, returned.reshape(-1, width))
    bits = n_feat // 2
    while bits > 1:
        part = part + crossed(part, "feat", bits)
        bits //= 2
    mine_gram, mine = gram_blocks(part, crossed(part, "feat", 1), place, n_feat)
    mine_gram = sum_over_dp(mine_gram)
    other_gram = crossed(mine_gram, "feat", 1)
    return whiten(mine_gram, other_gram, mine, place, s_dev * n_dp)


def solution(mesh):
    return jax.shard_map(
        local,
        mesh=mesh,
        in_specs=(P("feat", "dp", None, None), P("feat", "dp", None), P("dp", "feat", None, None)),
        out_specs=P(("dp", "feat"), None),
        check_vma=False,
    )
```

```python
import functools
import math

import jax
import jax.numpy as jnp
import numpy as np
from jax import lax
from jax.experimental import pallas as pl
from jax.experimental.pallas import tpu as pltpu
from jax.sharding import PartitionSpec as P

ridge = 0.1
root_steps = 4
f32 = jnp.float32
bf16 = jnp.bfloat16
lane = 128
chunk = 256
vmem_limit = 48 << 20

COLS = (((0,), (0,)), ((), ()))


def params(**kw):
    return pltpu.CompilerParams(vmem_limit_bytes=vmem_limit, **kw)


def whole():
    return pl.BlockSpec(memory_space=pltpu.VMEM)


def joint_of(per_dev):
    return math.gcd(per_dev, 4)


def pack_kernel(per_dev, bound, ids_ref, values_ref, send_ref, position_ref):
    k_j, s_dev = ids_ref.shape
    n_dp, slots, width = send_ref.shape
    n_ids = n_dp * per_dev
    joint = joint_of(per_dev)
    ids_rows = ids_ref[...]
    padded = jnp.concatenate([ids_rows.astype(f32), jnp.zeros((lane - k_j, s_dev), f32)], axis=0)
    ids_cols = jnp.transpose(padded)
    numbers = lax.broadcasted_iota(jnp.int32, (s_dev, n_ids), 1).astype(f32)
    number_rows = lax.broadcasted_iota(jnp.int32, (n_ids, s_dev), 0)
    earlier = (
        lax.broadcasted_iota(jnp.int32, (s_dev, s_dev), 0) > lax.broadcasted_iota(jnp.int32, (s_dev, s_dev), 1)
    )
    earlier = jnp.where(earlier, 1.0, 0.0).astype(bf16)
    used = jnp.zeros((1, n_ids), f32)
    total = jnp.zeros((n_ids, bound * width), f32)
    places = []
    for k in range(k_j):
        column = ids_cols[:, k : k + 1]
        named = jnp.where(column == numbers, 1.0, 0.0)
        before = jnp.dot(earlier, named.astype(bf16), preferred_element_type=f32) + used
        rank = jnp.sum(named * before, axis=1, keepdims=True)
        used = used + jnp.sum(named, axis=0, keepdims=True)
        tile = values_ref[:, k * width : (k + 1) * width].astype(f32)
        by_rank = jnp.concatenate([jnp.where(rank == r, tile, 0.0).astype(bf16) for r in range(bound)], axis=1)
        named_rows = jnp.where(ids_rows[k : k + 1, :] == number_rows, 1.0, 0.0).astype(bf16)
        total = total + jnp.dot(named_rows, by_rank, preferred_element_type=f32)
        id_col = column.astype(jnp.int32)
        group = id_col // joint
        places.append((group * bound + rank.astype(jnp.int32)) * joint + id_col - group * joint)
    position = jnp.concatenate(places + [jnp.zeros((s_dev, lane - k_j), jnp.int32)], axis=1).astype(f32)
    position_ref[...] = jnp.transpose(position)[: position_ref.shape[0]]
    slot = lax.broadcasted_iota(jnp.int32, (slots, slots), 0)
    origin = lax.broadcasted_iota(jnp.int32, (slots, slots), 1)
    group = slot // (joint * bound)
    rank = (slot - group * (joint * bound)) // joint
    block = group * joint + slot % joint
    order = jnp.where(origin == rank * per_dev + block, 1.0, 0.0).astype(bf16)
    for to in range(n_dp):
        rows = total[to * per_dev : (to + 1) * per_dev, :]
        rows = jnp.concatenate([rows[:, r * width : (r + 1) * width] for r in range(bound)], axis=0)
        send_ref[to] = jnp.dot(order, rows.astype(bf16), preferred_element_type=f32).astype(bf16)


def pack(ids, values, n_dp, per_dev, bound):
    k_j, s_dev = ids.shape
    return pl.pallas_call(
        functools.partial(pack_kernel, per_dev, bound),
        out_shape=(
            jax.ShapeDtypeStruct((n_dp, bound * per_dev, lane), bf16),
            jax.ShapeDtypeStruct((8, s_dev), f32),
        ),
        in_specs=[whole(), whole()],
        out_specs=(whole(), whole()),
        compiler_params=params(),
        name="pack",
    )(ids, values)


def product_kernel(bound, joint, groups, place_ref, tiles_ref, probe_ref, out_ref):
    inner, outer, unit, width = out_ref.shape
    count = inner * outer
    rows = bound * joint
    start = pl.multiple_of(pl.program_id(0) * unit, unit)
    place = place_ref[0]
    tiles = [
        tiles_ref[b * inner + (place ^ a), pl.ds(start, unit), :].astype(f32)
        for a in range(inner)
        for b in range(outer)
    ]
    own = lax.broadcasted_iota(jnp.int32, (count * rows, lane), 0) % joint
    parts = []
    for g in range(groups):
        tile = jnp.concatenate([t[g * rows : (g + 1) * rows] for t in tiles], axis=0)
        spread = jnp.concatenate([jnp.where(own == j, tile, 0.0).astype(bf16) for j in range(joint)], axis=1)
        probe = probe_ref[g * joint : (g + 1) * joint].reshape(joint * lane, width)
        parts.append(jnp.dot(spread, probe, preferred_element_type=f32))
    for a in range(inner):
        for b in range(outer):
            at = (a * outer + b) * rows
            value = jnp.concatenate([part[at : at + rows] for part in parts], axis=0)
            out_ref[a, b] = value.astype(bf16)


def product(place, tiles, probe, inner, bound, first, width):
    n_dp, slots, _ = tiles.shape
    per_dev = probe.shape[0]
    joint = joint_of(per_dev)
    groups = 1 if bound * joint % 16 == 0 else 2
    unit = groups * bound * joint
    return pl.pallas_call(
        functools.partial(product_kernel, bound, joint, groups),
        out_shape=jax.ShapeDtypeStruct((inner, n_dp // inner, slots, width), bf16),
        grid=(slots // unit,),
        in_specs=[
            pl.BlockSpec(memory_space=pltpu.SMEM),
            pl.BlockSpec((n_dp, slots, lane), lambda i: (0, 0, 0)),
            pl.BlockSpec((groups * joint, lane, width), lambda i: (i, 0, first // width)),
        ],
        out_specs=pl.BlockSpec((inner, n_dp // inner, unit, width), lambda i: (0, 0, i, 0)),
        compiler_params=params(),
        cost_estimate=pl.CostEstimate(flops=2 * n_dp * slots * joint * lane * width, bytes_accessed=1 << 22, transcendentals=0),
        name="product",
    )(place.reshape(1), tiles, probe)


def choose_kernel(k_j, slots, inner, place_ref, *refs):
    position_refs, out_ref = refs[:-1], refs[-1]
    _, s_dev, count = out_ref.shape
    place, outer_at = place_ref[0], place_ref[1]
    at = lax.broadcasted_iota(jnp.int32, (1, count), 1)
    expect = jnp.zeros((1, count), jnp.int32)
    for a in range(inner):
        inside = jnp.logical_and(at >= a * slots, at < (a + 1) * slots)
        expect = jnp.where(inside, (outer_at * inner + (place ^ a)) * slots + at - a * slots, expect)
    expect = expect.astype(f32)
    rows = [ref[...] for ref in position_refs]
    rows = jnp.concatenate(rows + [jnp.zeros((lane - 8 * len(rows), s_dev), f32)], axis=0)
    columns = jnp.transpose(rows)
    for c in range(len(position_refs)):
        hit = columns[:, 8 * c : 8 * c + 1] == expect
        for k in range(1, k_j):
            hit = jnp.logical_or(hit, columns[:, 8 * c + k : 8 * c + k + 1] == expect)
        out_ref[c] = jnp.where(hit, 1.0, 0.0).astype(bf16)


def choose(place, outer_at, positions, k_j, slots, inner):
    s_dev = positions[0].shape[1]
    return pl.pallas_call(
        functools.partial(choose_kernel, k_j, slots, inner),
        out_shape=jax.ShapeDtypeStruct((len(positions), s_dev, inner * slots), bf16),
        in_specs=[pl.BlockSpec(memory_space=pltpu.SMEM)] + [whole()] * len(positions),
        out_specs=whole(),
        compiler_params=params(),
        cost_estimate=pl.CostEstimate(flops=1 << 24, bytes_accessed=1 << 23, transcendentals=0),
        name="choose",
    )(jnp.stack([place, outer_at]), *positions)


def gather_kernel(outer, place_ref, hits_ref, *refs):
    rows_refs, keep_ref, give_ref = refs[:-2], refs[-2], refs[-1]
    half = keep_ref.shape[1]
    slots = rows_refs[0].shape[1]
    feat, outer_at = place_ref[0], place_ref[1]
    for c in range(outer):
        rows = jnp.concatenate([ref[outer_at ^ c] for ref in rows_refs], axis=0)
        give = hits_ref[c, pl.ds(pl.multiple_of((1 - feat) * half, half), half), :]
        give_ref[c] = jnp.dot(give, rows, preferred_element_type=f32).astype(bf16)
        keep = hits_ref[c, pl.ds(pl.multiple_of(feat * half, half), half), :]
        keep_ref[c] = jnp.dot(keep, rows, preferred_element_type=f32)


def gather(feat, outer_at, hits, rows):
    outer, s_dev, _ = hits.shape
    width = rows[0].shape[2]
    return pl.pallas_call(
        functools.partial(gather_kernel, outer),
        out_shape=(
            jax.ShapeDtypeStruct((outer, s_dev // 2, width), f32),
            jax.ShapeDtypeStruct((outer, s_dev // 2, width), bf16),
        ),
        in_specs=[pl.BlockSpec(memory_space=pltpu.SMEM)] + [whole()] * (1 + len(rows)),
        out_specs=(whole(), whole()),
        compiler_params=params(),
        cost_estimate=pl.CostEstimate(flops=2 * hits.size * width, bytes_accessed=1 << 23, transcendentals=0),
        name="gather",
    )(jnp.stack([feat, outer_at]), hits, *rows)


def combine_kernel(k_j, position_ref, rows_ref, out_ref):
    step = pl.program_id(0)
    s_dev = position_ref.shape[1]
    count = rows_ref.shape[0]
    here = lax.broadcasted_iota(jnp.int32, (s_dev, count), 1) + step * count
    rows = jnp.concatenate([position_ref[...], jnp.zeros((lane - 8, s_dev), f32)], axis=0)
    position = jnp.transpose(rows).astype(jnp.int32)
    hit = position[:, 0:1] == here
    for k in range(1, k_j):
        hit = jnp.logical_or(hit, position[:, k : k + 1] == here)
    part = jnp.dot(jnp.where(hit, 1.0, 0.0).astype(bf16), rows_ref[...], preferred_element_type=f32)

    @pl.when(step == 0)
    def _():
        out_ref[...] = part

    @pl.when(step > 0)
    def _():
        out_ref[...] += part


def combine(position, rows, k_j):
    s_dev = position.shape[1]
    total, width = rows.shape
    count = total // 6 if total % (6 * lane) == 0 else total
    return pl.pallas_call(
        functools.partial(combine_kernel, k_j),
        out_shape=jax.ShapeDtypeStruct((s_dev, width), f32),
        grid=(total // count,),
        in_specs=[
            pl.BlockSpec((8, s_dev), lambda i: (0, 0)),
            pl.BlockSpec((count, width), lambda i: (i, 0)),
        ],
        out_specs=pl.BlockSpec((s_dev, width), lambda i: (0, 0)),
        compiler_params=params(),
        name="combine",
    )(position, rows)


def block_pairs(width):
    n = width // lane
    return [(i, j) for i in range(n) for j in range(i, n)]


def gram_kernel(pairs_ref, sketch_ref, gram_ref):
    for at in range(gram_ref.shape[0]):
        left = sketch_ref[:, pl.ds(pl.multiple_of(pairs_ref[2 * at] * lane, lane), lane)]
        right = sketch_ref[:, pl.ds(pl.multiple_of(pairs_ref[2 * at + 1] * lane, lane), lane)]
        gram_ref[at] = lax.dot_general(left, right, COLS, preferred_element_type=f32)


def gram_blocks(sketch, feat):
    width = sketch.shape[1]
    pairs = block_pairs(width)
    half = len(pairs) // 2
    table = jnp.asarray(np.array(pairs, np.int32).reshape(2, 2 * half))
    smem = pl.BlockSpec(memory_space=pltpu.SMEM)
    return pl.pallas_call(
        gram_kernel,
        out_shape=jax.ShapeDtypeStruct((half, lane, lane), f32),
        in_specs=[smem, whole()],
        out_specs=whole(),
        compiler_params=params(),
        name="gram",
    )(table[feat % 2], sketch)


def halves(value):
    high = value.astype(bf16)
    return high, (value - high.astype(f32)).astype(bf16)


def dot3(a, b):
    (ah, al), (bh, bl) = a, b
    out = jnp.dot(ah, bl, preferred_element_type=f32)
    if al is not None:
        out = out + jnp.dot(al, bh, preferred_element_type=f32)
    return out + jnp.dot(ah, bh, preferred_element_type=f32)


def root_kernel(samples, place_ref, mine_gram_ref, other_gram_ref, mine_ref, out_ref, gram):
    width = mine_ref.shape[1]
    pairs = block_pairs(width)
    half = len(pairs) // 2
    odd = place_ref[0] % 2 == 1
    for at, (i, j) in enumerate(pairs):
        mine, other = mine_gram_ref[at % half], other_gram_ref[at % half]
        block = jnp.where(odd, other, mine) if at < half else jnp.where(odd, mine, other)
        gram[i * lane : (i + 1) * lane, j * lane : (j + 1) * lane] = block
        if i != j:
            gram[j * lane : (j + 1) * lane, i * lane : (i + 1) * lane] = jnp.transpose(block)
    rows = lax.broadcasted_iota(jnp.int32, (width, width), 0)
    ident = jnp.where(rows == lax.broadcasted_iota(jnp.int32, (width, width), 1), 1.0, 0.0)
    total = gram[...] + ridge * samples * ident
    scale = jnp.sum(total * ident, axis=(0, 1), keepdims=True) / width
    current = total / scale
    result = (mine_ref[...], None)
    for step in range(root_steps):
        middle = halves(1.5 * ident - 0.5 * current)
        if step + 1 < root_steps:
            current = dot3(halves(dot3(halves(current), middle)), middle)
        value = dot3(result, middle)
        result = halves(value)
    out_ref[...] = (math.sqrt(samples) * lax.rsqrt(scale)) * value


def whiten(mine_gram, other_gram, mine, place, samples):
    width = mine.shape[1]
    return pl.pallas_call(
        functools.partial(root_kernel, samples),
        out_shape=jax.ShapeDtypeStruct(mine.shape, f32),
        in_specs=[pl.BlockSpec(memory_space=pltpu.SMEM), whole(), whole(), whole()],
        out_specs=whole(),
        scratch_shapes=[pltpu.VMEM((width, width), f32)],
        compiler_params=params(),
        name="root",
    )(place.reshape(1), mine_gram, other_gram, mine)


def crossed(value, axis, bits):
    count = lax.axis_size(axis)
    return lax.ppermute(value, axis, [(source, source ^ bits) for source in range(count)])


def sum_over_dp(value):
    n_dp = lax.axis_size("dp")
    index = lax.axis_index("dp")
    inner = math.gcd(n_dp, 4)
    flat = value.reshape(-1, lane)
    rows = flat.shape[0] // inner
    me = index % inner
    part = lax.dynamic_slice_in_dim(flat, me * rows, rows, 0)
    arrived = [
        crossed(lax.dynamic_slice_in_dim(flat, (me ^ bits) * rows, rows, 0), "dp", bits) for bits in range(1, inner)
    ]
    for other in arrived:
        part = part + other
    if n_dp // inner == 4:
        arrived = [crossed(part, "dp", bits * inner) for bits in range(1, 4)]
        for other in arrived:
            part = part + other
    else:
        bits = inner
        while bits < n_dp:
            part = part + crossed(part, "dp", bits)
            bits *= 2
    pieces = [part] + [crossed(part, "dp", bits) for bits in range(1, inner)]
    stacked = jnp.stack(pieces)
    ordered = [stacked[me ^ at] for at in range(inner)]
    return jnp.concatenate(ordered, axis=0).reshape(value.shape)


def sketch_by_all_to_all(products, position, k_j):
    n_feat = lax.axis_size("feat")
    feat = lax.axis_index("feat")
    width = products.shape[2]
    returned = lax.all_to_all(products, "dp", split_axis=0, concat_axis=0, tiled=True)
    part = combine(position, returned.reshape(-1, width), k_j)
    bits = 1
    while bits < n_feat:
        part = part + crossed(part, "feat", bits)
        bits *= 2
    sketch = part.astype(bf16)
    own_rows = sketch.shape[0] // n_feat
    return lax.dynamic_slice_in_dim(sketch, feat * own_rows, own_rows, 0), sketch


def sketch_by_planes(tiles, probe, position, inner, bound, k_j):
    n_dp, slots, _ = tiles.shape
    outer = n_dp // inner
    index, feat = lax.axis_index("dp"), lax.axis_index("feat")
    place, outer_at = index % inner, index // inner
    width = probe.shape[2]
    positions = [position] + [crossed(position, "dp", c * inner) for c in range(1, outer)]
    hits = choose(place, outer_at, positions, k_j, slots, inner)
    mine, others = [], []
    for first in range(0, width, chunk):
        sent = product(place, tiles, probe, inner, bound, first, chunk)
        rows = [sent[0]] + [crossed(sent[a], "dp", a) for a in range(1, inner)]
        keep, give = gather(feat, outer_at, hits, rows)
        plane = keep + crossed(give, "feat", 1).astype(f32)
        total = plane[0]
        for c in range(1, outer):
            total = total + crossed(plane[c].astype(bf16), "dp", c * inner).astype(f32)
        mine.append(total.astype(bf16))
        others.append(crossed(mine[-1], "feat", 1))
    mine, others = jnp.concatenate(mine, axis=1), jnp.concatenate(others, axis=1)
    return mine, jnp.concatenate([mine, others], axis=0)


def local(grads, block_ids, probe):
    values = grads[0]
    s_dev, k_j, b_width = values.shape
    n_dp, n_feat = lax.axis_size("dp"), lax.axis_size("feat")
    feat = lax.axis_index("feat")
    per_dev = probe.shape[0]
    width = probe.shape[3]
    b_slice = per_dev * n_dp
    bound = max(2, 3 * s_dev * k_j // (2 * b_slice))
    probe = probe[:, 0]
    send, position = pack(block_ids[0].T, values.reshape(s_dev, k_j * b_width), n_dp, per_dev, bound)
    tiles = lax.all_to_all(send, "dp", split_axis=0, concat_axis=0, tiled=True)
    if n_feat == 2 and n_dp == 16:
        mine, sketch = sketch_by_planes(tiles, probe, position, 4, bound, k_j)
    else:
        products = product(jnp.zeros((), jnp.int32), tiles, probe, 1, bound, 0, width)
        mine, sketch = sketch_by_all_to_all(products[0], position, k_j)
    mine_gram = sum_over_dp(gram_blocks(sketch, feat))
    other_gram = crossed(mine_gram, "feat", 1)
    return whiten(mine_gram, other_gram, mine, feat, s_dev * n_dp)


def solution(mesh):
    return jax.shard_map(
        local,
        mesh=mesh,
        in_specs=(P("feat", "dp", None, None), P("feat", "dp", None), P("dp", "feat", None, None)),
        out_specs=P(("dp", "feat"), None),
        check_vma=False,
    )
```

```python
import functools
import math

import jax
import jax.numpy as jnp
import numpy as np
from jax import lax
from jax.experimental import pallas as pl
from jax.experimental.pallas import tpu as pltpu
from jax.sharding import PartitionSpec as P

ridge = 0.1
root_steps = 4
f32 = jnp.float32
bf16 = jnp.bfloat16
lane = 128
chunks = (256, 256)

COLS = (((0,), (0,)), ((), ()))


small = pl.CostEstimate(flops=1, bytes_accessed=1, transcendentals=0)


def params(limit=24 << 20):
    return pltpu.CompilerParams(vmem_limit_bytes=limit)


def whole():
    return pl.BlockSpec(memory_space=pltpu.VMEM)


def joint_of(per_dev):
    return math.gcd(per_dev, 4)


def pack_kernel(per_dev, bound, ids_ref, values_ref, send_ref, position_ref, values):
    k_j, s_dev = ids_ref.shape
    n_dp, slots, width = send_ref.shape
    n_ids = n_dp * per_dev
    joint = joint_of(per_dev)
    values[...] = values_ref[...].astype(f32)
    ids_rows = ids_ref[...]
    padded = jnp.concatenate([ids_rows.astype(f32), jnp.zeros((lane - k_j, s_dev), f32)], axis=0)
    ids_cols = jnp.transpose(padded)
    numbers = lax.broadcasted_iota(jnp.int32, (s_dev, n_ids), 1).astype(f32)
    number_rows = lax.broadcasted_iota(jnp.int32, (n_ids, s_dev), 0)
    earlier = (
        lax.broadcasted_iota(jnp.int32, (s_dev, s_dev), 0) > lax.broadcasted_iota(jnp.int32, (s_dev, s_dev), 1)
    )
    earlier = jnp.where(earlier, 1.0, 0.0).astype(bf16)
    used = jnp.zeros((1, n_ids), f32)
    places, by_rank, named_rows = [], [], []
    for k in range(k_j):
        column = ids_cols[:, k : k + 1]
        named = jnp.where(column == numbers, 1.0, 0.0)
        before = jnp.dot(earlier, named.astype(bf16), preferred_element_type=f32) + used
        rank = jnp.sum(named * before, axis=1, keepdims=True)
        used = used + jnp.sum(named, axis=0, keepdims=True)
        tile = values[pl.ds(k, s_dev, stride=k_j), :]
        by_rank.append(jnp.concatenate([jnp.where(rank == r, tile, 0.0).astype(bf16) for r in range(bound)], axis=1))
        named_rows.append(jnp.where(ids_rows[k : k + 1, :] == number_rows, 1.0, 0.0).astype(bf16))
        id_col = column.astype(jnp.int32)
        group = id_col // joint
        places.append((group * bound + rank.astype(jnp.int32)) * joint + id_col - group * joint)
    named_rows, by_rank = jnp.concatenate(named_rows, axis=1), jnp.concatenate(by_rank, axis=0)
    total = jnp.dot(named_rows, by_rank, preferred_element_type=f32).astype(bf16)
    position = jnp.concatenate(places + [jnp.zeros((s_dev, lane - k_j), jnp.int32)], axis=1).astype(f32)
    position_ref[...] = jnp.transpose(position)[: position_ref.shape[0]]
    slot = lax.broadcasted_iota(jnp.int32, (slots, slots), 0)
    origin = lax.broadcasted_iota(jnp.int32, (slots, slots), 1)
    group = slot // (joint * bound)
    rank = (slot - group * (joint * bound)) // joint
    block = group * joint + slot % joint
    order = jnp.where(origin == rank * per_dev + block, 1.0, 0.0).astype(bf16)
    rows = [
        jnp.concatenate(
            [total[to * per_dev : (to + 1) * per_dev, r * width : (r + 1) * width] for r in range(bound)], axis=0
        )
        for to in range(n_dp)
    ]
    out = jnp.dot(order, jnp.concatenate(rows, axis=1), preferred_element_type=f32).astype(bf16)
    for to in range(n_dp):
        send_ref[to] = out[:, to * width : (to + 1) * width]


def pack(ids, values, n_dp, per_dev, bound):
    k_j, s_dev = ids.shape
    return pl.pallas_call(
        functools.partial(pack_kernel, per_dev, bound),
        out_shape=(
            jax.ShapeDtypeStruct((n_dp, bound * per_dev, lane), bf16),
            jax.ShapeDtypeStruct((8, s_dev), f32),
        ),
        in_specs=[whole(), whole()],
        out_specs=(whole(), whole()),
        scratch_shapes=[pltpu.VMEM(values.shape, f32)],
        compiler_params=params(),
        name="pack",
    )(ids, values)


def product_kernel(bound, joint, groups, place_ref, tiles_ref, probe_ref, *out_refs):
    inner = len(out_refs)
    outer, _, width = out_refs[0].shape
    count = inner * outer
    rows = bound * joint
    unit = groups * bound * joint
    start = pl.multiple_of(pl.program_id(0) * unit, unit)
    place = place_ref[0]
    tiles = [
        tiles_ref[b * inner + (place ^ a), pl.ds(start, unit), :].astype(f32)
        for a in range(inner)
        for b in range(outer)
    ]
    own = lax.broadcasted_iota(jnp.int32, (count * rows, lane), 0) % joint
    parts = []
    for g in range(groups):
        tile = jnp.concatenate([t[g * rows : (g + 1) * rows] for t in tiles], axis=0)
        spread = jnp.concatenate([jnp.where(own == j, tile, 0.0).astype(bf16) for j in range(joint)], axis=1)
        probe = probe_ref[g * joint : (g + 1) * joint].reshape(joint * lane, width)
        parts.append(jnp.dot(spread, probe, preferred_element_type=f32))
    for a in range(inner):
        for b in range(outer):
            at = (a * outer + b) * rows
            value = jnp.concatenate([part[at : at + rows] for part in parts], axis=0)
            out_refs[a][b, pl.ds(start, unit), :] = value.astype(bf16)


def product(place, tiles, probe, inner, bound, first, width):
    n_dp, slots, _ = tiles.shape
    per_dev = probe.shape[0]
    joint = joint_of(per_dev)
    groups = 1 if bound * joint % 16 == 0 else 2
    unit = groups * bound * joint
    return pl.pallas_call(
        functools.partial(product_kernel, bound, joint, groups),
        out_shape=[jax.ShapeDtypeStruct((n_dp // inner, slots, width), bf16)] * inner,
        grid=(slots // unit,),
        in_specs=[
            pl.BlockSpec(memory_space=pltpu.SMEM),
            whole(),
            pl.BlockSpec((groups * joint, lane, width), lambda i: (i, 0, first // width)),
        ],
        out_specs=[whole()] * inner,
        compiler_params=params(48 << 20),
        cost_estimate=small,
        name="product",
    )(place.reshape(1), tiles, probe)


def choose_kernel(k_j, slots, inner, place_ref, *refs):
    position_refs, out_ref = refs[:-1], refs[-1]
    _, s_dev, count = out_ref.shape
    place, outer_at = place_ref[0], place_ref[1]
    at = lax.broadcasted_iota(jnp.int32, (1, count), 1)
    expect = jnp.zeros((1, count), jnp.int32)
    for a in range(inner):
        inside = jnp.logical_and(at >= a * slots, at < (a + 1) * slots)
        expect = jnp.where(inside, (outer_at * inner + (place ^ a)) * slots + at - a * slots, expect)
    expect = expect.astype(f32)
    rows = [ref[...] for ref in position_refs]
    rows = jnp.concatenate(rows + [jnp.zeros((lane - 8 * len(rows), s_dev), f32)], axis=0)
    columns = jnp.transpose(rows)
    for c in range(len(position_refs)):
        hit = columns[:, 8 * c : 8 * c + 1] == expect
        for k in range(1, k_j):
            hit = jnp.logical_or(hit, columns[:, 8 * c + k : 8 * c + k + 1] == expect)
        out_ref[c] = jnp.where(hit, 1.0, 0.0).astype(bf16)


def choose(place, outer_at, positions, k_j, slots, inner):
    s_dev = positions[0].shape[1]
    return pl.pallas_call(
        functools.partial(choose_kernel, k_j, slots, inner),
        out_shape=jax.ShapeDtypeStruct((len(positions), s_dev, inner * slots), bf16),
        in_specs=[pl.BlockSpec(memory_space=pltpu.SMEM)] + [whole()] * len(positions),
        out_specs=whole(),
        compiler_params=params(),
        cost_estimate=small,
        name="choose",
    )(jnp.stack([place, outer_at]), *positions)


def gather_kernel(pieces, place_ref, hits_ref, *refs):
    count = len(pieces)
    rows_refs, keep_refs, give_refs = refs[: -2 * count], refs[-2 * count : -count], refs[-count:]
    half = hits_ref.shape[1] // 2
    feat, outer_at = place_ref[0], place_ref[1]
    for piece, keep_ref, give_ref in zip(pieces, keep_refs, give_refs, strict=True):
        for at, c in enumerate(piece):
            rows = jnp.concatenate([ref[outer_at ^ c] for ref in rows_refs], axis=0)
            give = hits_ref[c, pl.ds(pl.multiple_of((1 - feat) * half, half), half), :]
            give_ref[at] = jnp.dot(give, rows, preferred_element_type=f32).astype(bf16)
            keep = hits_ref[c, pl.ds(pl.multiple_of(feat * half, half), half), :]
            keep_ref[at] = jnp.dot(keep, rows, preferred_element_type=f32)


def gather(feat, outer_at, hits, rows, pieces):
    half, width = hits.shape[1] // 2, rows[0].shape[2]
    shapes = [(len(piece), half, width) for piece in pieces]
    count = len(pieces)
    out = pl.pallas_call(
        functools.partial(gather_kernel, pieces),
        out_shape=[jax.ShapeDtypeStruct(shape, kind) for kind in (f32, bf16) for shape in shapes],
        in_specs=[pl.BlockSpec(memory_space=pltpu.SMEM)] + [whole()] * (1 + len(rows)),
        out_specs=[whole()] * (2 * count),
        compiler_params=params(),
        cost_estimate=small,
        name="gather",
    )(jnp.stack([feat, outer_at]), hits, *rows)
    return out[:count], out[count:]


def combine_kernel(k_j, position_ref, rows_ref, out_ref):
    step = pl.program_id(0)
    s_dev = position_ref.shape[1]
    count = rows_ref.shape[0]
    here = lax.broadcasted_iota(jnp.int32, (s_dev, count), 1) + step * count
    rows = jnp.concatenate([position_ref[...], jnp.zeros((lane - 8, s_dev), f32)], axis=0)
    position = jnp.transpose(rows).astype(jnp.int32)
    hit = position[:, 0:1] == here
    for k in range(1, k_j):
        hit = jnp.logical_or(hit, position[:, k : k + 1] == here)
    part = jnp.dot(jnp.where(hit, 1.0, 0.0).astype(bf16), rows_ref[...], preferred_element_type=f32)

    @pl.when(step == 0)
    def _():
        out_ref[...] = part

    @pl.when(step > 0)
    def _():
        out_ref[...] += part


def combine(position, rows, k_j):
    s_dev = position.shape[1]
    total, width = rows.shape
    count = total // 6 if total % (6 * lane) == 0 else total
    return pl.pallas_call(
        functools.partial(combine_kernel, k_j),
        out_shape=jax.ShapeDtypeStruct((s_dev, width), f32),
        grid=(total // count,),
        in_specs=[
            pl.BlockSpec((8, s_dev), lambda i: (0, 0)),
            pl.BlockSpec((count, width), lambda i: (i, 0)),
        ],
        out_specs=pl.BlockSpec((s_dev, width), lambda i: (0, 0)),
        compiler_params=params(),
        name="combine",
    )(position, rows)


def block_pairs(width):
    n = width // lane
    return [(i, j) for i in range(n) for j in range(i, n)]


def gram_kernel(pairs_ref, sketch_ref, gram_ref):
    for at in range(gram_ref.shape[0]):
        left = sketch_ref[:, pl.ds(pl.multiple_of(pairs_ref[2 * at] * lane, lane), lane)]
        right = sketch_ref[:, pl.ds(pl.multiple_of(pairs_ref[2 * at + 1] * lane, lane), lane)]
        gram_ref[at] = lax.dot_general(left, right, COLS, preferred_element_type=f32).astype(bf16)


def gram_blocks(sketch, feat):
    width = sketch.shape[1]
    pairs = block_pairs(width)
    half = len(pairs) // 2
    table = jnp.asarray(np.array(pairs, np.int32).reshape(2, 2 * half))
    smem = pl.BlockSpec(memory_space=pltpu.SMEM)
    return pl.pallas_call(
        gram_kernel,
        out_shape=jax.ShapeDtypeStruct((half, lane, lane), bf16),
        in_specs=[smem, whole()],
        out_specs=whole(),
        compiler_params=params(),
        name="gram",
    )(table[feat % 2], sketch)


def halves(value):
    high = value.astype(bf16)
    return high, (value - high.astype(f32)).astype(bf16)


def dot3(a, b):
    (ah, al), (bh, bl) = a, b
    out = jnp.dot(ah, bl, preferred_element_type=f32)
    if al is not None:
        out = out + jnp.dot(al, bh, preferred_element_type=f32)
    return out + jnp.dot(ah, bh, preferred_element_type=f32)


def root_kernel(samples, place_ref, mine_gram_ref, other_gram_ref, mine_ref, out_ref, gram):
    width = mine_ref.shape[1]
    pairs = block_pairs(width)
    half = len(pairs) // 2
    odd = place_ref[0] % 2 == 1
    for at, (i, j) in enumerate(pairs):
        mine, other = mine_gram_ref[at % half].astype(f32), other_gram_ref[at % half].astype(f32)
        block = jnp.where(odd == (at < half), other, mine)
        gram[i * lane : (i + 1) * lane, j * lane : (j + 1) * lane] = block
        if i != j:
            gram[j * lane : (j + 1) * lane, i * lane : (i + 1) * lane] = jnp.transpose(block)
    rows = lax.broadcasted_iota(jnp.int32, (width, width), 0)
    ident = jnp.where(rows == lax.broadcasted_iota(jnp.int32, (width, width), 1), 1.0, 0.0)
    total = gram[...] + ridge * samples * ident
    scale = jnp.sum(total * ident, axis=(0, 1), keepdims=True) / width
    current = total / scale
    result = (mine_ref[...], None)
    for step in range(root_steps):
        middle = halves(1.5 * ident - 0.5 * current)
        if step + 1 < root_steps:
            current = dot3(halves(dot3(halves(current), middle)), middle)
        value = dot3(result, middle)
        result = halves(value)
    out_ref[...] = (math.sqrt(samples) * lax.rsqrt(scale)) * value


def whiten(mine_gram, other_gram, mine, place, samples):
    width = mine.shape[1]
    return pl.pallas_call(
        functools.partial(root_kernel, samples),
        out_shape=jax.ShapeDtypeStruct(mine.shape, f32),
        in_specs=[pl.BlockSpec(memory_space=pltpu.SMEM), whole(), whole(), whole()],
        out_specs=whole(),
        scratch_shapes=[pltpu.VMEM((width, width), f32)],
        compiler_params=params(),
        name="root",
    )(place.reshape(1), mine_gram, other_gram, mine)


def crossed(value, axis, bits):
    count = lax.axis_size(axis)
    return lax.ppermute(value, axis, [(source, source ^ bits) for source in range(count)])


def total_of(values):
    total = values[0].astype(f32)
    for value in values[1:]:
        total = total + value.astype(f32)
    return total


def sum_over_dp(value):
    n_dp = lax.axis_size("dp")
    inner = math.gcd(n_dp, 4)
    me = lax.axis_index("dp") & (inner - 1)
    flat = value.reshape(-1, lane)
    rows = flat.shape[0] // inner
    parts = [lax.dynamic_slice_in_dim(flat, (me ^ bits) * rows, rows, 0) for bits in range(inner)]
    part = total_of([parts[0]] + [crossed(parts[bits], "dp", bits) for bits in range(1, inner)]).astype(bf16)
    if n_dp // inner == 4:
        part = total_of([part] + [crossed(part, "dp", bits * inner) for bits in range(1, 4)]).astype(bf16)
    else:
        bits = inner
        while bits < n_dp:
            part = total_of([part, crossed(part, "dp", bits)]).astype(bf16)
            bits *= 2
    pieces = jnp.stack([part] + [crossed(part, "dp", bits) for bits in range(1, inner)])
    return jnp.concatenate([pieces[me ^ at] for at in range(inner)], axis=0).reshape(value.shape)


def sketch_by_all_to_all(products, position, k_j):
    n_feat = lax.axis_size("feat")
    feat = lax.axis_index("feat")
    width = products.shape[2]
    returned = lax.all_to_all(products, "dp", split_axis=0, concat_axis=0, tiled=True)
    part = combine(position, returned.reshape(-1, width), k_j)
    bits = 1
    while bits < n_feat:
        part = part + crossed(part, "feat", bits)
        bits *= 2
    sketch = part.astype(bf16)
    own_rows = sketch.shape[0] // n_feat
    return lax.dynamic_slice_in_dim(sketch, feat * own_rows, own_rows, 0), sketch


def sketch_by_planes(tiles, probe, position, inner, bound, k_j):
    n_dp, slots, _ = tiles.shape
    outer = n_dp // inner
    index, feat = lax.axis_index("dp"), lax.axis_index("feat")
    place, outer_at = index % inner, index // inner
    width = probe.shape[2]
    positions = [position] + [crossed(position, "dp", c * inner) for c in range(1, outer)]
    mine, others, before = [], [], None
    firsts = [sum(chunks[:at]) for at in range(len(chunks))]
    sent = [product(place, tiles, probe, inner, bound, first, size) for first, size in zip(firsts, chunks, strict=True)]
    arrived = [[block[0]] + [crossed(block[a], "dp", a) for a in range(1, inner)] for block in sent]
    positions, _ = lax.optimization_barrier((positions, sent))
    hits = choose(place, outer_at, positions, k_j, slots, inner)
    for at, rows in enumerate(arrived):
        if at > 0:
            rows, _ = lax.optimization_barrier((rows, before))
        last = at + 1 == len(sent)
        pieces = [(3, 2, 1), (0,)] if last else [(c,) for c in range(outer - 1, -1, -1)]
        keep, give = gather(feat, outer_at, hits, rows, pieces)
        plane = {}
        for piece, a, b in zip(pieces, keep, give, strict=True):
            both = a + crossed(b, "feat", 1).astype(f32)
            plane.update({c: both[at] for at, c in enumerate(piece)})
        plane = [plane[c] for c in range(outer)]
        if not last:
            size = 1
            while size < outer:
                away = [crossed(one.astype(bf16), "dp", size * inner) for one in plane[1::2]]
                plane = [total_of(pair) for pair in zip(plane[0::2], away, strict=True)]
                size *= 2
            plane = before = plane[0]
        else:
            plane = total_of([plane[0]] + [crossed(plane[c].astype(bf16), "dp", c * inner) for c in range(1, outer)])
        mine.append(plane.astype(bf16))
        others.append(crossed(mine[-1], "feat", 1))
    mine, others = jnp.concatenate(mine, axis=1), jnp.concatenate(others, axis=1)
    return mine, jnp.concatenate([mine, others], axis=0)


def local(grads, block_ids, probe):
    values = grads[0]
    s_dev, k_j, b_width = values.shape
    n_dp, n_feat = lax.axis_size("dp"), lax.axis_size("feat")
    feat = lax.axis_index("feat")
    per_dev = probe.shape[0]
    width = probe.shape[3]
    b_slice = per_dev * n_dp
    bound = max(2, 3 * s_dev * k_j // (2 * b_slice))
    probe = probe[:, 0]
    send, position = pack(block_ids[0].T, values.reshape(s_dev * k_j, b_width), n_dp, per_dev, bound)
    tiles = lax.all_to_all(send, "dp", split_axis=0, concat_axis=0, tiled=True)
    if n_feat == 2 and n_dp == 16:
        mine, sketch = sketch_by_planes(tiles, probe, position, 4, bound, k_j)
    else:
        products = product(jnp.zeros((), jnp.int32), tiles, probe, 1, bound, 0, width)
        mine, sketch = sketch_by_all_to_all(products[0], position, k_j)
    mine_gram = sum_over_dp(gram_blocks(sketch, feat))
    other_gram = crossed(mine_gram, "feat", 1)
    return whiten(mine_gram, other_gram, mine, feat, s_dev * n_dp)


def solution(mesh):
    return jax.shard_map(
        local,
        mesh=mesh,
        in_specs=(P("feat", "dp", None, None), P("feat", "dp", None), P("dp", "feat", None, None)),
        out_specs=P(("dp", "feat"), None),
        check_vma=False,
    )
```

```python
import functools
import math

import jax
import jax.numpy as jnp
import numpy as np
from jax import lax
from jax.experimental import pallas as pl
from jax.experimental.pallas import tpu as pltpu
from jax.sharding import PartitionSpec as P

ridge = 0.1
root_steps = 4
f32 = jnp.float32
bf16 = jnp.bfloat16
lane = 128
stages = ((3,), (2,), (1,), (0,))

COLS = (((0,), (0,)), ((), ()))


large = pl.CostEstimate(flops=1 << 34, bytes_accessed=1, transcendentals=0)
small = pl.CostEstimate(flops=1, bytes_accessed=1, transcendentals=0)


def params(limit=24 << 20):
    return pltpu.CompilerParams(vmem_limit_bytes=limit)


def whole():
    return pl.BlockSpec(memory_space=pltpu.VMEM)


def joint_of(per_dev):
    return math.gcd(per_dev, 4)


def pack_kernel(per_dev, bound, ids_ref, values_ref, send_ref, position_ref, values):
    k_j, s_dev = ids_ref.shape
    n_dp, slots, width = send_ref.shape
    n_ids = n_dp * per_dev
    joint = joint_of(per_dev)
    values[...] = values_ref[...].astype(f32)
    ids_rows = ids_ref[...]
    padded = jnp.concatenate([ids_rows.astype(f32), jnp.zeros((lane - k_j, s_dev), f32)], axis=0)
    ids_cols = jnp.transpose(padded)
    numbers = lax.broadcasted_iota(jnp.int32, (s_dev, n_ids), 1).astype(f32)
    number_rows = lax.broadcasted_iota(jnp.int32, (n_ids, s_dev), 0)
    earlier = (
        lax.broadcasted_iota(jnp.int32, (s_dev, s_dev), 0) > lax.broadcasted_iota(jnp.int32, (s_dev, s_dev), 1)
    )
    earlier = jnp.where(earlier, 1.0, 0.0).astype(bf16)
    used = jnp.zeros((1, n_ids), f32)
    places, by_rank, named_rows = [], [], []
    for k in range(k_j):
        column = ids_cols[:, k : k + 1]
        named = jnp.where(column == numbers, 1.0, 0.0)
        before = jnp.dot(earlier, named.astype(bf16), preferred_element_type=f32) + used
        rank = jnp.sum(named * before, axis=1, keepdims=True)
        used = used + jnp.sum(named, axis=0, keepdims=True)
        tile = values[pl.ds(k, s_dev, stride=k_j), :]
        by_rank.append(jnp.concatenate([jnp.where(rank == r, tile, 0.0).astype(bf16) for r in range(bound)], axis=1))
        named_rows.append(jnp.where(ids_rows[k : k + 1, :] == number_rows, 1.0, 0.0).astype(bf16))
        id_col = column.astype(jnp.int32)
        group = id_col // joint
        places.append((group * bound + rank.astype(jnp.int32)) * joint + id_col - group * joint)
    named_rows, by_rank = jnp.concatenate(named_rows, axis=1), jnp.concatenate(by_rank, axis=0)
    total = jnp.dot(named_rows, by_rank, preferred_element_type=f32).astype(bf16)
    position = jnp.concatenate(places + [jnp.zeros((s_dev, lane - k_j), jnp.int32)], axis=1).astype(f32)
    position_ref[...] = jnp.transpose(position)[: position_ref.shape[0]]
    slot = lax.broadcasted_iota(jnp.int32, (slots, slots), 0)
    origin = lax.broadcasted_iota(jnp.int32, (slots, slots), 1)
    group = slot // (joint * bound)
    rank = (slot - group * (joint * bound)) // joint
    block = group * joint + slot % joint
    order = jnp.where(origin == rank * per_dev + block, 1.0, 0.0).astype(bf16)
    rows = [
        jnp.concatenate(
            [total[to * per_dev : (to + 1) * per_dev, r * width : (r + 1) * width] for r in range(bound)], axis=0
        )
        for to in range(n_dp)
    ]
    out = jnp.dot(order, jnp.concatenate(rows, axis=1), preferred_element_type=f32).astype(bf16)
    for to in range(n_dp):
        send_ref[to] = out[:, to * width : (to + 1) * width]


def pack(ids, values, n_dp, per_dev, bound):
    k_j, s_dev = ids.shape
    return pl.pallas_call(
        functools.partial(pack_kernel, per_dev, bound),
        out_shape=(
            jax.ShapeDtypeStruct((n_dp, bound * per_dev, lane), bf16),
            jax.ShapeDtypeStruct((8, s_dev), f32),
        ),
        in_specs=[whole(), whole()],
        out_specs=(whole(), whole()),
        scratch_shapes=[pltpu.VMEM(values.shape, f32)],
        compiler_params=params(),
        name="pack",
    )(ids, values)


def product_kernel(bound, joint, groups, away, where_ref, tiles_ref, probe_ref, *out_refs):
    inner = len(out_refs)
    width = out_refs[0].shape[2]
    count = inner * len(away)
    rows = bound * joint
    unit = groups * rows
    blocks = groups * joint
    units = probe_ref.shape[0] // blocks
    place, outer_at = where_ref[0], where_ref[1]
    own = lax.broadcasted_iota(jnp.int32, (count * rows, lane), 0) % joint
    for u in range(units):
        tiles = [
            tiles_ref[(outer_at ^ b) * inner + (place ^ a), u * unit : (u + 1) * unit, :].astype(f32)
            for a in range(inner)
            for b in away
        ]
        parts = []
        for g in range(groups):
            tile = jnp.concatenate([t[g * rows : (g + 1) * rows] for t in tiles], axis=0)
            spread = jnp.concatenate([jnp.where(own == j, tile, 0.0).astype(bf16) for j in range(joint)], axis=1)
            first = u * blocks + g * joint
            probe = probe_ref[first : first + joint].reshape(joint * lane, width)
            parts.append(jnp.dot(spread, probe, preferred_element_type=f32))
        for a in range(inner):
            for b in range(len(away)):
                at = (a * len(away) + b) * rows
                value = jnp.concatenate([part[at : at + rows] for part in parts], axis=0)
                out_refs[a][b, u * unit : (u + 1) * unit, :] = value.astype(bf16)


def product(where, tiles, probe, inner, bound, away):
    n_dp, slots, _ = tiles.shape
    per_dev, _, width = probe.shape
    joint = joint_of(per_dev)
    groups = 1 if bound * joint % 16 == 0 else 2
    return pl.pallas_call(
        functools.partial(product_kernel, bound, joint, groups, away),
        out_shape=[jax.ShapeDtypeStruct((len(away), slots, width), bf16)] * inner,
        in_specs=[pl.BlockSpec(memory_space=pltpu.SMEM), whole(), whole()],
        out_specs=[whole()] * inner,
        compiler_params=params(),
        cost_estimate=large,
        name="product",
    )(where, tiles, probe)


def choose_kernel(k_j, slots, inner, place_ref, *refs):
    position_refs, out_ref = refs[:-1], refs[-1]
    _, s_dev, count = out_ref.shape
    place, outer_at = place_ref[0], place_ref[1]
    at = lax.broadcasted_iota(jnp.int32, (1, count), 1)
    expect = jnp.zeros((1, count), jnp.int32)
    for a in range(inner):
        inside = jnp.logical_and(at >= a * slots, at < (a + 1) * slots)
        expect = jnp.where(inside, (outer_at * inner + (place ^ a)) * slots + at - a * slots, expect)
    expect = expect.astype(f32)
    rows = [ref[...] for ref in position_refs]
    rows = jnp.concatenate(rows + [jnp.zeros((lane - 8 * len(rows), s_dev), f32)], axis=0)
    columns = jnp.transpose(rows)
    for c in range(len(position_refs)):
        hit = columns[:, 8 * c : 8 * c + 1] == expect
        for k in range(1, k_j):
            hit = jnp.logical_or(hit, columns[:, 8 * c + k : 8 * c + k + 1] == expect)
        out_ref[c] = jnp.where(hit, 1.0, 0.0).astype(bf16)


def choose(where, positions, k_j, slots, inner):
    s_dev = positions[0].shape[1]
    return pl.pallas_call(
        functools.partial(choose_kernel, k_j, slots, inner),
        out_shape=jax.ShapeDtypeStruct((len(positions), s_dev, inner * slots), bf16),
        in_specs=[pl.BlockSpec(memory_space=pltpu.SMEM)] + [whole()] * len(positions),
        out_specs=whole(),
        compiler_params=params(),
        cost_estimate=large,
        name="choose",
    )(where, *positions)


def gather_kernel(away, feat_ref, hits_ref, *refs):
    rows_refs, (keep_ref, give_ref) = refs[:-2], refs[-2:]
    half = hits_ref.shape[1] // 2
    keep_at = pl.multiple_of(feat_ref[0] * half, half)
    give_at = pl.multiple_of((1 - feat_ref[0]) * half, half)
    for at, c in enumerate(away):
        rows = jnp.concatenate([ref[at] for ref in rows_refs], axis=0)
        give_ref[at] = jnp.dot(hits_ref[c, pl.ds(give_at, half), :], rows, preferred_element_type=f32).astype(bf16)
        keep_ref[at] = jnp.dot(hits_ref[c, pl.ds(keep_at, half), :], rows, preferred_element_type=f32)


def gather(feat, hits, rows, away):
    shape = (len(away), hits.shape[1] // 2, rows[0].shape[2])
    return pl.pallas_call(
        functools.partial(gather_kernel, away),
        out_shape=(jax.ShapeDtypeStruct(shape, f32), jax.ShapeDtypeStruct(shape, bf16)),
        in_specs=[pl.BlockSpec(memory_space=pltpu.SMEM)] + [whole()] * (1 + len(rows)),
        out_specs=(whole(), whole()),
        compiler_params=params(),
        cost_estimate=large,
        name="gather",
    )(feat.reshape(1), hits, *rows)


def combine_kernel(k_j, position_ref, rows_ref, out_ref):
    step = pl.program_id(0)
    s_dev = position_ref.shape[1]
    count = rows_ref.shape[0]
    here = lax.broadcasted_iota(jnp.int32, (s_dev, count), 1) + step * count
    rows = jnp.concatenate([position_ref[...], jnp.zeros((lane - 8, s_dev), f32)], axis=0)
    position = jnp.transpose(rows).astype(jnp.int32)
    hit = position[:, 0:1] == here
    for k in range(1, k_j):
        hit = jnp.logical_or(hit, position[:, k : k + 1] == here)
    part = jnp.dot(jnp.where(hit, 1.0, 0.0).astype(bf16), rows_ref[...], preferred_element_type=f32)

    @pl.when(step == 0)
    def _():
        out_ref[...] = part

    @pl.when(step > 0)
    def _():
        out_ref[...] += part


def combine(position, rows, k_j):
    s_dev = position.shape[1]
    total, width = rows.shape
    count = total // 6 if total % (6 * lane) == 0 else total
    return pl.pallas_call(
        functools.partial(combine_kernel, k_j),
        out_shape=jax.ShapeDtypeStruct((s_dev, width), f32),
        grid=(total // count,),
        in_specs=[
            pl.BlockSpec((8, s_dev), lambda i: (0, 0)),
            pl.BlockSpec((count, width), lambda i: (i, 0)),
        ],
        out_specs=pl.BlockSpec((s_dev, width), lambda i: (0, 0)),
        compiler_params=params(),
        name="combine",
    )(position, rows)


def block_pairs(width):
    n = width // lane
    return [(i, j) for i in range(n) for j in range(i, n)]


def gram_kernel(pairs_ref, sketch_ref, gram_ref):
    for at in range(gram_ref.shape[0]):
        left = sketch_ref[:, pl.ds(pl.multiple_of(pairs_ref[2 * at] * lane, lane), lane)]
        right = sketch_ref[:, pl.ds(pl.multiple_of(pairs_ref[2 * at + 1] * lane, lane), lane)]
        gram_ref[at] = lax.dot_general(left, right, COLS, preferred_element_type=f32).astype(bf16)


def gram_blocks(sketch, feat):
    width = sketch.shape[1]
    pairs = block_pairs(width)
    half = len(pairs) // 2
    table = jnp.asarray(np.array(pairs, np.int32).reshape(2, 2 * half))
    smem = pl.BlockSpec(memory_space=pltpu.SMEM)
    return pl.pallas_call(
        gram_kernel,
        out_shape=jax.ShapeDtypeStruct((half, lane, lane), bf16),
        in_specs=[smem, whole()],
        out_specs=whole(),
        compiler_params=params(),
        name="gram",
    )(table[feat % 2], sketch)


def halves(value):
    high = value.astype(bf16)
    return high, (value - high.astype(f32)).astype(bf16)


def dot3(a, b):
    (ah, al), (bh, bl) = a, b
    out = jnp.dot(ah, bl, preferred_element_type=f32)
    if al is not None:
        out = out + jnp.dot(al, bh, preferred_element_type=f32)
    return out + jnp.dot(ah, bh, preferred_element_type=f32)


def root_kernel(samples, place_ref, mine_gram_ref, other_gram_ref, mine_ref, out_ref, gram):
    width = mine_ref.shape[1]
    pairs = block_pairs(width)
    half = len(pairs) // 2
    odd = place_ref[0] % 2 == 1
    for at, (i, j) in enumerate(pairs):
        mine, other = mine_gram_ref[at % half].astype(f32), other_gram_ref[at % half].astype(f32)
        block = jnp.where(odd == (at < half), other, mine)
        gram[i * lane : (i + 1) * lane, j * lane : (j + 1) * lane] = block
        if i != j:
            gram[j * lane : (j + 1) * lane, i * lane : (i + 1) * lane] = jnp.transpose(block)
    rows = lax.broadcasted_iota(jnp.int32, (width, width), 0)
    ident = jnp.where(rows == lax.broadcasted_iota(jnp.int32, (width, width), 1), 1.0, 0.0)
    total = gram[...] + ridge * samples * ident
    scale = jnp.sum(total * ident, axis=(0, 1), keepdims=True) / width
    current = total / scale
    result = (mine_ref[...], None)
    for step in range(root_steps):
        middle = halves(1.5 * ident - 0.5 * current)
        if step + 1 < root_steps:
            current = dot3(halves(dot3(halves(current), middle)), middle)
        value = dot3(result, middle)
        result = halves(value)
    out_ref[...] = (math.sqrt(samples) * lax.rsqrt(scale)) * value


def whiten(mine_gram, other_gram, mine, place, samples):
    width = mine.shape[1]
    return pl.pallas_call(
        functools.partial(root_kernel, samples),
        out_shape=jax.ShapeDtypeStruct(mine.shape, f32),
        in_specs=[pl.BlockSpec(memory_space=pltpu.SMEM), whole(), whole(), whole()],
        out_specs=whole(),
        scratch_shapes=[pltpu.VMEM((width, width), f32)],
        compiler_params=params(),
        name="root",
    )(place.reshape(1), mine_gram, other_gram, mine)


def crossed(value, axis, bits):
    count = lax.axis_size(axis)
    return lax.ppermute(value, axis, [(source, source ^ bits) for source in range(count)])


def total_of(values):
    total = values[0].astype(f32)
    for value in values[1:]:
        total = total + value.astype(f32)
    return total


def sum_over_dp(value):
    n_dp = lax.axis_size("dp")
    inner = math.gcd(n_dp, 4)
    me = lax.axis_index("dp") & (inner - 1)
    flat = value.reshape(-1, lane)
    rows = flat.shape[0] // inner
    parts = [lax.dynamic_slice_in_dim(flat, (me ^ bits) * rows, rows, 0) for bits in range(inner)]
    part = total_of([parts[0]] + [crossed(parts[bits], "dp", bits) for bits in range(1, inner)]).astype(bf16)
    if n_dp // inner == 4:
        part = total_of([part] + [crossed(part, "dp", bits * inner) for bits in range(1, 4)]).astype(bf16)
    else:
        bits = inner
        while bits < n_dp:
            part = total_of([part, crossed(part, "dp", bits)]).astype(bf16)
            bits *= 2
    pieces = jnp.stack([part] + [crossed(part, "dp", bits) for bits in range(1, inner)])
    return jnp.concatenate([pieces[me ^ at] for at in range(inner)], axis=0).reshape(value.shape)


def sketch_by_all_to_all(products, position, k_j):
    n_feat = lax.axis_size("feat")
    feat = lax.axis_index("feat")
    width = products.shape[2]
    returned = lax.all_to_all(products, "dp", split_axis=0, concat_axis=0, tiled=True)
    part = combine(position, returned.reshape(-1, width), k_j)
    bits = 1
    while bits < n_feat:
        part = part + crossed(part, "feat", bits)
        bits *= 2
    sketch = part.astype(bf16)
    own_rows = sketch.shape[0] // n_feat
    return lax.dynamic_slice_in_dim(sketch, feat * own_rows, own_rows, 0), sketch


def tied(value, *others):
    return lax.optimization_barrier((value, others))[0]


def sketch_by_planes(tiles, probe, position, inner, bound, k_j):
    n_dp, slots, _ = tiles.shape
    index, feat = lax.axis_index("dp"), lax.axis_index("feat")
    where = jnp.stack([index & (inner - 1), index // inner])
    positions = [position] + [crossed(position, "dp", c * inner) for c in range(1, n_dp // inner)]
    sent = []
    for at, away in enumerate(stages):
        behind = sent[-1] if at else positions
        sent.append(product(where, tied(tiles, behind), probe, inner, bound, away))
    hits = choose(where, tied(positions, sent[-1]), k_j, slots, inner)
    plane, kept, behind = {}, [], None
    for at, away in enumerate(stages):
        rows = [sent[at][0]] + [crossed(sent[at][a], "dp", a) for a in range(1, inner)]
        if at:
            rows = tied(rows, kept[-1], plane[2] if at == 2 else kept[-1])
        keep, give = gather(feat, hits, rows, away)
        kept.append(keep)
        both = keep + crossed(give, "feat", 1).astype(f32)
        plane.update({c: both[i] for i, c in enumerate(away)})
        if at == 1:
            plane[2] = plane[2] + crossed(plane[3].astype(bf16), "dp", inner).astype(f32)
    plane[0] = plane[0] + crossed(plane[1].astype(bf16), "dp", inner).astype(f32)
    mine = (plane[0] + crossed(plane[2].astype(bf16), "dp", 2 * inner).astype(f32)).astype(bf16)
    return mine, jnp.concatenate([mine, crossed(mine, "feat", 1)], axis=0)


def local(grads, block_ids, probe):
    values = grads[0]
    s_dev, k_j, b_width = values.shape
    n_dp, n_feat = lax.axis_size("dp"), lax.axis_size("feat")
    feat = lax.axis_index("feat")
    per_dev = probe.shape[0]
    width = probe.shape[3]
    b_slice = per_dev * n_dp
    bound = max(2, 3 * s_dev * k_j // (2 * b_slice))
    probe = probe[:, 0]
    send, position = pack(block_ids[0].T, values.reshape(s_dev * k_j, b_width), n_dp, per_dev, bound)
    tiles = lax.all_to_all(send, "dp", split_axis=0, concat_axis=0, tiled=True)
    if n_feat == 2 and n_dp == 16:
        mine, sketch = sketch_by_planes(tiles, probe, position, 4, bound, k_j)
    else:
        products = product(jnp.zeros((2,), jnp.int32), tiles, probe, 1, bound, tuple(range(n_dp)))
        mine, sketch = sketch_by_all_to_all(products[0], position, k_j)
    mine_gram = sum_over_dp(gram_blocks(sketch, feat))
    other_gram = crossed(mine_gram, "feat", 1)
    return whiten(mine_gram, other_gram, mine, feat, s_dev * n_dp)


def solution(mesh):
    return jax.shard_map(
        local,
        mesh=mesh,
        in_specs=(P("feat", "dp", None, None), P("feat", "dp", None), P("dp", "feat", None, None)),
        out_specs=P(("dp", "feat"), None),
        check_vma=False,
    )
```

```python
import functools
import math

import jax
import jax.numpy as jnp
import numpy as np
from jax import lax
from jax.experimental import pallas as pl
from jax.experimental.pallas import tpu as pltpu
from jax.sharding import PartitionSpec as P

ridge = 0.1
root_steps = 4
f32 = jnp.float32
bf16 = jnp.bfloat16
lane = 128
stages = ((3,), (2,), (1,), (0,))

COLS = (((0,), (0,)), ((), ()))


large = pl.CostEstimate(flops=1 << 34, bytes_accessed=1, transcendentals=0)
small = pl.CostEstimate(flops=1, bytes_accessed=1, transcendentals=0)


def params(limit=24 << 20):
    return pltpu.CompilerParams(vmem_limit_bytes=limit)


def whole():
    return pl.BlockSpec(memory_space=pltpu.VMEM)


def joint_of(per_dev):
    return math.gcd(per_dev, 4)


def pack_kernel(per_dev, bound, ids_ref, values_ref, send_ref, position_ref, values, raw, arrived):
    k_j, s_dev = ids_ref.shape
    n_dp, slots, width = send_ref.shape
    n_ids = n_dp * per_dev
    joint = joint_of(per_dev)
    copy = pltpu.make_async_copy(values_ref, raw, arrived)
    copy.start()
    ids_rows = ids_ref[...]
    padded = jnp.concatenate([ids_rows.astype(f32), jnp.zeros((lane - k_j, s_dev), f32)], axis=0)
    ids_cols = jnp.transpose(padded)
    numbers = lax.broadcasted_iota(jnp.int32, (s_dev, n_ids), 1).astype(f32)
    number_rows = lax.broadcasted_iota(jnp.int32, (n_ids, s_dev), 0)
    earlier = (
        lax.broadcasted_iota(jnp.int32, (s_dev, s_dev), 0) > lax.broadcasted_iota(jnp.int32, (s_dev, s_dev), 1)
    )
    earlier = jnp.where(earlier, 1.0, 0.0).astype(bf16)
    used = jnp.zeros((1, n_ids), f32)
    places, by_rank, named_rows = [], [], []
    for k in range(k_j):
        column = ids_cols[:, k : k + 1]
        named = jnp.where(column == numbers, 1.0, 0.0)
        before = jnp.dot(earlier, named.astype(bf16), preferred_element_type=f32) + used
        rank = jnp.sum(named * before, axis=1, keepdims=True)
        used = used + jnp.sum(named, axis=0, keepdims=True)
        if k == 0:
            copy.wait()
            values[...] = raw[...].astype(f32)
        tile = values[pl.ds(k, s_dev, stride=k_j), :]
        by_rank.append(jnp.concatenate([jnp.where(rank == r, tile, 0.0).astype(bf16) for r in range(bound)], axis=1))
        named_rows.append(jnp.where(ids_rows[k : k + 1, :] == number_rows, 1.0, 0.0).astype(bf16))
        id_col = column.astype(jnp.int32)
        group = id_col // joint
        places.append((group * bound + rank.astype(jnp.int32)) * joint + id_col - group * joint)
    named_rows, by_rank = jnp.concatenate(named_rows, axis=1), jnp.concatenate(by_rank, axis=0)
    total = jnp.dot(named_rows, by_rank, preferred_element_type=f32).astype(bf16)
    position = jnp.concatenate(places + [jnp.zeros((s_dev, lane - k_j), jnp.int32)], axis=1).astype(f32)
    position_ref[...] = jnp.transpose(position)[: position_ref.shape[0]]
    slot = lax.broadcasted_iota(jnp.int32, (slots, slots), 0)
    origin = lax.broadcasted_iota(jnp.int32, (slots, slots), 1)
    group = slot // (joint * bound)
    rank = (slot - group * (joint * bound)) // joint
    block = group * joint + slot % joint
    order = jnp.where(origin == rank * per_dev + block, 1.0, 0.0).astype(bf16)
    rows = [
        jnp.concatenate(
            [total[to * per_dev : (to + 1) * per_dev, r * width : (r + 1) * width] for r in range(bound)], axis=0
        )
        for to in range(n_dp)
    ]
    out = jnp.dot(order, jnp.concatenate(rows, axis=1), preferred_element_type=f32).astype(bf16)
    for to in range(n_dp):
        send_ref[to] = out[:, to * width : (to + 1) * width]


def pack(ids, values, n_dp, per_dev, bound):
    k_j, s_dev = ids.shape
    return pl.pallas_call(
        functools.partial(pack_kernel, per_dev, bound),
        out_shape=(
            jax.ShapeDtypeStruct((n_dp, bound * per_dev, lane), bf16),
            jax.ShapeDtypeStruct((8, s_dev), f32),
        ),
        in_specs=[whole(), pl.BlockSpec(memory_space=pl.ANY)],
        out_specs=(whole(), whole()),
        scratch_shapes=[pltpu.VMEM(values.shape, f32), pltpu.VMEM(values.shape, bf16), pltpu.SemaphoreType.DMA],
        compiler_params=params(62 << 20),
        name="pack",
    )(ids, values)


def product_kernel(bound, joint, groups, away, where_ref, tiles_ref, probe_ref, *out_refs):
    inner = len(out_refs)
    width = out_refs[0].shape[2]
    count = inner * len(away)
    rows = bound * joint
    unit = groups * rows
    blocks = groups * joint
    units = probe_ref.shape[0] // blocks
    place, outer_at = where_ref[0], where_ref[1]
    own = lax.broadcasted_iota(jnp.int32, (count * rows, lane), 0) % joint
    for u in range(units):
        tiles = [
            tiles_ref[(outer_at ^ b) * inner + (place ^ a), u * unit : (u + 1) * unit, :].astype(f32)
            for a in range(inner)
            for b in away
        ]
        parts = []
        for g in range(groups):
            tile = jnp.concatenate([t[g * rows : (g + 1) * rows] for t in tiles], axis=0)
            spread = jnp.concatenate([jnp.where(own == j, tile, 0.0).astype(bf16) for j in range(joint)], axis=1)
            first = u * blocks + g * joint
            probe = probe_ref[first : first + joint].reshape(joint * lane, width)
            parts.append(jnp.dot(spread, probe, preferred_element_type=f32))
        for a in range(inner):
            for b in range(len(away)):
                at = (a * len(away) + b) * rows
                value = jnp.concatenate([part[at : at + rows] for part in parts], axis=0)
                out_refs[a][b, u * unit : (u + 1) * unit, :] = value.astype(bf16)


def product(where, tiles, probe, inner, bound, away):
    n_dp, slots, _ = tiles.shape
    per_dev, _, width = probe.shape
    joint = joint_of(per_dev)
    groups = 1 if bound * joint % 16 == 0 else 2
    return pl.pallas_call(
        functools.partial(product_kernel, bound, joint, groups, away),
        out_shape=[jax.ShapeDtypeStruct((len(away), slots, width), bf16)] * inner,
        in_specs=[pl.BlockSpec(memory_space=pltpu.SMEM), whole(), whole()],
        out_specs=[whole()] * inner,
        compiler_params=params(),
        cost_estimate=large,
        name="product",
    )(where, tiles, probe)


def choose_kernel(k_j, slots, inner, place_ref, *refs):
    position_refs, out_ref = refs[:-1], refs[-1]
    _, s_dev, count = out_ref.shape
    place, outer_at = place_ref[0], place_ref[1]
    at = lax.broadcasted_iota(jnp.int32, (1, count), 1)
    expect = jnp.zeros((1, count), jnp.int32)
    for a in range(inner):
        inside = jnp.logical_and(at >= a * slots, at < (a + 1) * slots)
        expect = jnp.where(inside, (outer_at * inner + (place ^ a)) * slots + at - a * slots, expect)
    expect = expect.astype(f32)
    rows = [ref[...] for ref in position_refs]
    rows = jnp.concatenate(rows + [jnp.zeros((lane - 8 * len(rows), s_dev), f32)], axis=0)
    columns = jnp.transpose(rows)
    for c in range(len(position_refs)):
        hit = columns[:, 8 * c : 8 * c + 1] == expect
        for k in range(1, k_j):
            hit = jnp.logical_or(hit, columns[:, 8 * c + k : 8 * c + k + 1] == expect)
        out_ref[c] = jnp.where(hit, 1.0, 0.0).astype(bf16)


def choose(where, positions, k_j, slots, inner):
    s_dev = positions[0].shape[1]
    return pl.pallas_call(
        functools.partial(choose_kernel, k_j, slots, inner),
        out_shape=jax.ShapeDtypeStruct((len(positions), s_dev, inner * slots), bf16),
        in_specs=[pl.BlockSpec(memory_space=pltpu.SMEM)] + [whole()] * len(positions),
        out_specs=whole(),
        compiler_params=params(),
        cost_estimate=large,
        name="choose",
    )(where, *positions)


def gather_kernel(away, feat_ref, hits_ref, *refs):
    rows_refs, (keep_ref, give_ref) = refs[:-2], refs[-2:]
    half = hits_ref.shape[1] // 2
    keep_at = pl.multiple_of(feat_ref[0] * half, half)
    give_at = pl.multiple_of((1 - feat_ref[0]) * half, half)
    for at, c in enumerate(away):
        rows = jnp.concatenate([ref[at] for ref in rows_refs], axis=0)
        give_ref[at] = jnp.dot(hits_ref[c, pl.ds(give_at, half), :], rows, preferred_element_type=f32).astype(bf16)
        keep_ref[at] = jnp.dot(hits_ref[c, pl.ds(keep_at, half), :], rows, preferred_element_type=f32)


def gather(feat, hits, rows, away):
    shape = (len(away), hits.shape[1] // 2, rows[0].shape[2])
    return pl.pallas_call(
        functools.partial(gather_kernel, away),
        out_shape=(jax.ShapeDtypeStruct(shape, f32), jax.ShapeDtypeStruct(shape, bf16)),
        in_specs=[pl.BlockSpec(memory_space=pltpu.SMEM)] + [whole()] * (1 + len(rows)),
        out_specs=(whole(), whole()),
        compiler_params=params(),
        cost_estimate=large,
        name="gather",
    )(feat.reshape(1), hits, *rows)


def combine_kernel(k_j, position_ref, rows_ref, out_ref):
    step = pl.program_id(0)
    s_dev = position_ref.shape[1]
    count = rows_ref.shape[0]
    here = lax.broadcasted_iota(jnp.int32, (s_dev, count), 1) + step * count
    rows = jnp.concatenate([position_ref[...], jnp.zeros((lane - 8, s_dev), f32)], axis=0)
    position = jnp.transpose(rows).astype(jnp.int32)
    hit = position[:, 0:1] == here
    for k in range(1, k_j):
        hit = jnp.logical_or(hit, position[:, k : k + 1] == here)
    part = jnp.dot(jnp.where(hit, 1.0, 0.0).astype(bf16), rows_ref[...], preferred_element_type=f32)

    @pl.when(step == 0)
    def _():
        out_ref[...] = part

    @pl.when(step > 0)
    def _():
        out_ref[...] += part


def combine(position, rows, k_j):
    s_dev = position.shape[1]
    total, width = rows.shape
    count = total // 6 if total % (6 * lane) == 0 else total
    return pl.pallas_call(
        functools.partial(combine_kernel, k_j),
        out_shape=jax.ShapeDtypeStruct((s_dev, width), f32),
        grid=(total // count,),
        in_specs=[
            pl.BlockSpec((8, s_dev), lambda i: (0, 0)),
            pl.BlockSpec((count, width), lambda i: (i, 0)),
        ],
        out_specs=pl.BlockSpec((s_dev, width), lambda i: (0, 0)),
        compiler_params=params(),
        name="combine",
    )(position, rows)


def block_pairs(width):
    n = width // lane
    return [(i, j) for i in range(n) for j in range(i, n)]


def gram_kernel(pairs_ref, sketch_ref, gram_ref):
    for at in range(gram_ref.shape[0]):
        left = sketch_ref[:, pl.ds(pl.multiple_of(pairs_ref[2 * at] * lane, lane), lane)]
        right = sketch_ref[:, pl.ds(pl.multiple_of(pairs_ref[2 * at + 1] * lane, lane), lane)]
        gram_ref[at] = lax.dot_general(left, right, COLS, preferred_element_type=f32).astype(bf16)


def gram_blocks(sketch, feat):
    width = sketch.shape[1]
    pairs = block_pairs(width)
    half = len(pairs) // 2
    table = jnp.asarray(np.array(pairs, np.int32).reshape(2, 2 * half))
    smem = pl.BlockSpec(memory_space=pltpu.SMEM)
    return pl.pallas_call(
        gram_kernel,
        out_shape=jax.ShapeDtypeStruct((half, lane, lane), bf16),
        in_specs=[smem, whole()],
        out_specs=whole(),
        compiler_params=params(),
        name="gram",
    )(table[feat % 2], sketch)


def halves(value):
    high = value.astype(bf16)
    return high, (value - high.astype(f32)).astype(bf16)


def left(value):
    high, low = halves(value)
    return jnp.concatenate([low, high, high], axis=1)


def right(value):
    high, low = halves(value)
    return jnp.concatenate([high, low, high], axis=0)


def dot3(a, b):
    return jnp.dot(a, b, preferred_element_type=f32)


def root_kernel(samples, place_ref, mine_gram_ref, other_gram_ref, mine_ref, out_ref, gram):
    width = mine_ref.shape[1]
    pairs = block_pairs(width)
    half = len(pairs) // 2
    odd = place_ref[0] % 2 == 1
    for at, (i, j) in enumerate(pairs):
        mine, other = mine_gram_ref[at % half].astype(f32), other_gram_ref[at % half].astype(f32)
        block = jnp.where(odd == (at < half), other, mine)
        gram[i * lane : (i + 1) * lane, j * lane : (j + 1) * lane] = block
        if i != j:
            gram[j * lane : (j + 1) * lane, i * lane : (i + 1) * lane] = jnp.transpose(block)
    rows = lax.broadcasted_iota(jnp.int32, (width, width), 0)
    ident = jnp.where(rows == lax.broadcasted_iota(jnp.int32, (width, width), 1), 1.0, 0.0)
    total = gram[...] + ridge * samples * ident
    scale = jnp.sum(total * ident, axis=(0, 1), keepdims=True) / width
    current = total / scale
    mine = mine_ref[...]
    for step in range(root_steps - 1):
        middle = 1.5 * ident - 0.5 * current
        by = right(middle)
        if step == 0:
            value = dot3(jnp.concatenate([mine, mine], axis=1), by[width:])
        else:
            value = dot3(left(value), by)
        if step + 2 < root_steps:
            current = dot3(left(dot3(left(current), by)), by)
    moved = dot3(left(dot3(left(dot3(left(value), right(current))), by)), by)
    value = 1.5 * value - 0.5 * moved
    out_ref[...] = (math.sqrt(samples) * lax.rsqrt(scale)) * value


def whiten(mine_gram, other_gram, mine, place, samples):
    width = mine.shape[1]
    return pl.pallas_call(
        functools.partial(root_kernel, samples),
        out_shape=jax.ShapeDtypeStruct(mine.shape, f32),
        in_specs=[pl.BlockSpec(memory_space=pltpu.SMEM), whole(), whole(), whole()],
        out_specs=whole(),
        scratch_shapes=[pltpu.VMEM((width, width), f32)],
        compiler_params=params(),
        name="root",
    )(place.reshape(1), mine_gram, other_gram, mine)


def crossed(value, axis, bits):
    count = lax.axis_size(axis)
    return lax.ppermute(value, axis, [(source, source ^ bits) for source in range(count)])


def total_of(values):
    total = values[0].astype(f32)
    for value in values[1:]:
        total = total + value.astype(f32)
    return total


def sum_over_dp(value):
    n_dp = lax.axis_size("dp")
    inner = math.gcd(n_dp, 4)
    me = lax.axis_index("dp") & (inner - 1)
    flat = value.reshape(-1, lane)
    rows = flat.shape[0] // inner
    parts = [lax.dynamic_slice_in_dim(flat, (me ^ bits) * rows, rows, 0) for bits in range(inner)]
    part = total_of([parts[0]] + [crossed(parts[bits], "dp", bits) for bits in range(1, inner)]).astype(bf16)
    if n_dp // inner == 4:
        part = total_of([part] + [crossed(part, "dp", bits * inner) for bits in range(1, 4)]).astype(bf16)
    else:
        bits = inner
        while bits < n_dp:
            part = total_of([part, crossed(part, "dp", bits)]).astype(bf16)
            bits *= 2
    pieces = jnp.stack([part] + [crossed(part, "dp", bits) for bits in range(1, inner)])
    return jnp.concatenate([pieces[me ^ at] for at in range(inner)], axis=0).reshape(value.shape)


def sketch_by_all_to_all(products, position, k_j):
    n_feat = lax.axis_size("feat")
    feat = lax.axis_index("feat")
    width = products.shape[2]
    returned = lax.all_to_all(products, "dp", split_axis=0, concat_axis=0, tiled=True)
    part = combine(position, returned.reshape(-1, width), k_j)
    bits = 1
    while bits < n_feat:
        part = part + crossed(part, "feat", bits)
        bits *= 2
    sketch = part.astype(bf16)
    own_rows = sketch.shape[0] // n_feat
    return lax.dynamic_slice_in_dim(sketch, feat * own_rows, own_rows, 0), sketch


def tied(value, *others):
    return lax.optimization_barrier((value, others))[0]


def sketch_by_planes(tiles, probe, position, inner, bound, k_j):
    n_dp, slots, _ = tiles.shape
    index, feat = lax.axis_index("dp"), lax.axis_index("feat")
    where = jnp.stack([index & (inner - 1), index // inner])
    positions = [position] + [crossed(position, "dp", c * inner) for c in range(1, n_dp // inner)]
    sent, hits = [], None
    for at, away in enumerate(stages):
        behind = positions if not at else sent[-1]
        if at == 2:
            hits = choose(where, tied(positions, sent[-1]), k_j, slots, inner)
            behind = hits
        sent.append(product(where, tied(tiles, behind), probe, inner, bound, away))
    plane, kept, behind = {}, [], None
    for at, away in enumerate(stages):
        rows = [sent[at][0]] + [crossed(sent[at][a], "dp", a) for a in range(1, inner)]
        if at:
            rows = tied(rows, kept[-1], (plane[3], sent[3]) if at == 2 else (plane[2], plane[1]) if at == 3 else kept[-1])
        keep, give = gather(feat, hits, rows, away)
        kept.append(keep)
        both = keep + crossed(give, "feat", 1).astype(f32)
        plane.update({c: both[i] for i, c in enumerate(away)})
        if at == 1:
            plane[2] = plane[2] + crossed(plane[3].astype(bf16), "dp", inner).astype(f32)
    plane[0] = plane[0] + crossed(plane[1].astype(bf16), "dp", inner).astype(f32)
    mine = (plane[0] + crossed(plane[2].astype(bf16), "dp", 2 * inner).astype(f32)).astype(bf16)
    return mine, jnp.concatenate([mine, crossed(mine, "feat", 1)], axis=0)


def local(grads, block_ids, probe):
    values = grads[0]
    s_dev, k_j, b_width = values.shape
    n_dp, n_feat = lax.axis_size("dp"), lax.axis_size("feat")
    feat = lax.axis_index("feat")
    per_dev = probe.shape[0]
    width = probe.shape[3]
    b_slice = per_dev * n_dp
    bound = max(2, 3 * s_dev * k_j // (2 * b_slice))
    probe = probe[:, 0]
    send, position = pack(block_ids[0].T, values.reshape(s_dev * k_j, b_width), n_dp, per_dev, bound)
    tiles = lax.all_to_all(send, "dp", split_axis=0, concat_axis=0, tiled=True)
    if n_feat == 2 and n_dp == 16:
        mine, sketch = sketch_by_planes(tiles, probe, position, 4, bound, k_j)
    else:
        products = product(jnp.zeros((2,), jnp.int32), tiles, probe, 1, bound, tuple(range(n_dp)))
        mine, sketch = sketch_by_all_to_all(products[0], position, k_j)
    mine_gram = sum_over_dp(gram_blocks(sketch, feat))
    other_gram = crossed(mine_gram, "feat", 1)
    return whiten(mine_gram, other_gram, mine, feat, s_dev * n_dp)


def solution(mesh):
    return jax.shard_map(
        local,
        mesh=mesh,
        in_specs=(P("feat", "dp", None, None), P("feat", "dp", None), P("dp", "feat", None, None)),
        out_specs=P(("dp", "feat"), None),
        check_vma=False,
    )
```

```python
import functools
import math

import jax
import jax.numpy as jnp
import numpy as np
from jax import lax
from jax.experimental import pallas as pl
from jax.experimental.pallas import tpu as pltpu
from jax.sharding import PartitionSpec as P

ridge = 0.1
root_steps = 4
f32 = jnp.float32
bf16 = jnp.bfloat16
lane = 128
stages = ((3,), (2,), (1,), (0,))

COLS = (((0,), (0,)), ((), ()))


large = pl.CostEstimate(flops=1 << 34, bytes_accessed=1, transcendentals=0)
small = pl.CostEstimate(flops=1, bytes_accessed=1, transcendentals=0)


def params(limit=24 << 20):
    return pltpu.CompilerParams(vmem_limit_bytes=limit)


def whole():
    return pl.BlockSpec(memory_space=pltpu.VMEM)


def joint_of(per_dev):
    return math.gcd(per_dev, 4)


def pack_kernel(per_dev, bound, ids_ref, values_ref, send_ref, position_ref, values, raw, arrived):
    k_j, s_dev = ids_ref.shape
    n_dp, slots, width = send_ref.shape
    n_ids = n_dp * per_dev
    joint = joint_of(per_dev)
    copy = pltpu.make_async_copy(values_ref, raw, arrived)
    copy.start()
    ids_rows = ids_ref[...]
    padded = jnp.concatenate([ids_rows.astype(f32), jnp.zeros((lane - k_j, s_dev), f32)], axis=0)
    ids_cols = jnp.transpose(padded)
    numbers = lax.broadcasted_iota(jnp.int32, (s_dev, n_ids), 1).astype(f32)
    number_rows = lax.broadcasted_iota(jnp.int32, (n_ids, s_dev), 0)
    earlier = (
        lax.broadcasted_iota(jnp.int32, (s_dev, s_dev), 0) > lax.broadcasted_iota(jnp.int32, (s_dev, s_dev), 1)
    )
    earlier = jnp.where(earlier, 1.0, 0.0).astype(bf16)
    used = jnp.zeros((1, n_ids), f32)
    places, by_rank, named_rows = [], [], []
    for k in range(k_j):
        column = ids_cols[:, k : k + 1]
        named = jnp.where(column == numbers, 1.0, 0.0)
        before = jnp.dot(earlier, named.astype(bf16), preferred_element_type=f32) + used
        rank = jnp.sum(named * before, axis=1, keepdims=True)
        used = used + jnp.sum(named, axis=0, keepdims=True)
        if k == 0:
            copy.wait()
            values[...] = raw[...].astype(f32)
        tile = values[pl.ds(k, s_dev, stride=k_j), :]
        by_rank.append(jnp.concatenate([jnp.where(rank == r, tile, 0.0).astype(bf16) for r in range(bound)], axis=1))
        named_rows.append(jnp.where(ids_rows[k : k + 1, :] == number_rows, 1.0, 0.0).astype(bf16))
        id_col = column.astype(jnp.int32)
        group = id_col // joint
        places.append((group * bound + rank.astype(jnp.int32)) * joint + id_col - group * joint)
    named_rows, by_rank = jnp.concatenate(named_rows, axis=1), jnp.concatenate(by_rank, axis=0)
    total = jnp.dot(named_rows, by_rank, preferred_element_type=f32).astype(bf16)
    position = jnp.concatenate(places + [jnp.zeros((s_dev, lane - k_j), jnp.int32)], axis=1).astype(f32)
    position_ref[...] = jnp.transpose(position)[: position_ref.shape[0]]
    slot = lax.broadcasted_iota(jnp.int32, (slots, slots), 0)
    origin = lax.broadcasted_iota(jnp.int32, (slots, slots), 1)
    group = slot // (joint * bound)
    rank = (slot - group * (joint * bound)) // joint
    block = group * joint + slot % joint
    order = jnp.where(origin == rank * per_dev + block, 1.0, 0.0).astype(bf16)
    rows = [
        jnp.concatenate(
            [total[to * per_dev : (to + 1) * per_dev, r * width : (r + 1) * width] for r in range(bound)], axis=0
        )
        for to in range(n_dp)
    ]
    out = jnp.dot(order, jnp.concatenate(rows, axis=1), preferred_element_type=f32).astype(bf16)
    for to in range(n_dp):
        send_ref[to] = out[:, to * width : (to + 1) * width]


def pack(ids, values, n_dp, per_dev, bound):
    k_j, s_dev = ids.shape
    return pl.pallas_call(
        functools.partial(pack_kernel, per_dev, bound),
        out_shape=(
            jax.ShapeDtypeStruct((n_dp, bound * per_dev, lane), bf16),
            jax.ShapeDtypeStruct((8, s_dev), f32),
        ),
        in_specs=[whole(), pl.BlockSpec(memory_space=pl.ANY)],
        out_specs=(whole(), whole()),
        scratch_shapes=[pltpu.VMEM(values.shape, f32), pltpu.VMEM(values.shape, bf16), pltpu.SemaphoreType.DMA],
        compiler_params=params(62 << 20),
        name="pack",
    )(ids, values)


def product_kernel(bound, joint, groups, away, where_ref, tiles_ref, probe_ref, *out_refs):
    inner = len(out_refs)
    width = out_refs[0].shape[2]
    count = inner * len(away)
    rows = bound * joint
    unit = groups * rows
    blocks = groups * joint
    units = probe_ref.shape[0] // blocks
    place, outer_at = where_ref[0], where_ref[1]
    own = lax.broadcasted_iota(jnp.int32, (count * rows, lane), 0) % joint
    for u in range(units):
        tiles = [
            tiles_ref[(outer_at ^ b) * inner + (place ^ a), u * unit : (u + 1) * unit, :].astype(f32)
            for a in range(inner)
            for b in away
        ]
        parts = []
        for g in range(groups):
            tile = jnp.concatenate([t[g * rows : (g + 1) * rows] for t in tiles], axis=0)
            spread = jnp.concatenate([jnp.where(own == j, tile, 0.0).astype(bf16) for j in range(joint)], axis=1)
            first = u * blocks + g * joint
            probe = probe_ref[first : first + joint].reshape(joint * lane, width)
            parts.append(jnp.dot(spread, probe, preferred_element_type=f32))
        for a in range(inner):
            for b in range(len(away)):
                at = (a * len(away) + b) * rows
                value = jnp.concatenate([part[at : at + rows] for part in parts], axis=0)
                out_refs[a][b, u * unit : (u + 1) * unit, :] = value.astype(bf16)


def product(where, tiles, probe, inner, bound, away):
    n_dp, slots, _ = tiles.shape
    per_dev, _, width = probe.shape
    joint = joint_of(per_dev)
    groups = 1 if bound * joint % 16 == 0 else 2
    return pl.pallas_call(
        functools.partial(product_kernel, bound, joint, groups, away),
        out_shape=[jax.ShapeDtypeStruct((len(away), slots, width), bf16)] * inner,
        in_specs=[pl.BlockSpec(memory_space=pltpu.SMEM), whole(), whole()],
        out_specs=[whole()] * inner,
        compiler_params=params(),
        cost_estimate=large,
        name="product",
    )(where, tiles, probe)


def choose_kernel(k_j, slots, inner, place_ref, *refs):
    position_refs, out_ref = refs[:-1], refs[-1]
    _, s_dev, count = out_ref.shape
    place, outer_at = place_ref[0], place_ref[1]
    at = lax.broadcasted_iota(jnp.int32, (1, count), 1)
    expect = jnp.zeros((1, count), jnp.int32)
    for a in range(inner):
        inside = jnp.logical_and(at >= a * slots, at < (a + 1) * slots)
        expect = jnp.where(inside, (outer_at * inner + (place ^ a)) * slots + at - a * slots, expect)
    expect = expect.astype(f32)
    rows = [ref[...] for ref in position_refs]
    rows = jnp.concatenate(rows + [jnp.zeros((lane - 8 * len(rows), s_dev), f32)], axis=0)
    columns = jnp.transpose(rows)
    for c in range(len(position_refs)):
        hit = columns[:, 8 * c : 8 * c + 1] == expect
        for k in range(1, k_j):
            hit = jnp.logical_or(hit, columns[:, 8 * c + k : 8 * c + k + 1] == expect)
        out_ref[c] = jnp.where(hit, 1.0, 0.0).astype(bf16)


def choose(where, positions, k_j, slots, inner):
    s_dev = positions[0].shape[1]
    return pl.pallas_call(
        functools.partial(choose_kernel, k_j, slots, inner),
        out_shape=jax.ShapeDtypeStruct((len(positions), s_dev, inner * slots), bf16),
        in_specs=[pl.BlockSpec(memory_space=pltpu.SMEM)] + [whole()] * len(positions),
        out_specs=whole(),
        compiler_params=params(),
        cost_estimate=large,
        name="choose",
    )(where, *positions)


def gather_kernel(away, feat_ref, hits_ref, *refs):
    rows_refs, (keep_ref, give_ref) = refs[:-2], refs[-2:]
    half = hits_ref.shape[1] // 2
    keep_at = pl.multiple_of(feat_ref[0] * half, half)
    give_at = pl.multiple_of((1 - feat_ref[0]) * half, half)
    for at, c in enumerate(away):
        rows = jnp.concatenate([ref[at] for ref in rows_refs], axis=0)
        give_ref[at] = jnp.dot(hits_ref[c, pl.ds(give_at, half), :], rows, preferred_element_type=f32).astype(bf16)
        keep_ref[at] = jnp.dot(hits_ref[c, pl.ds(keep_at, half), :], rows, preferred_element_type=f32)


def gather(feat, hits, rows, away):
    shape = (len(away), hits.shape[1] // 2, rows[0].shape[2])
    return pl.pallas_call(
        functools.partial(gather_kernel, away),
        out_shape=(jax.ShapeDtypeStruct(shape, f32), jax.ShapeDtypeStruct(shape, bf16)),
        in_specs=[pl.BlockSpec(memory_space=pltpu.SMEM)] + [whole()] * (1 + len(rows)),
        out_specs=(whole(), whole()),
        compiler_params=params(),
        cost_estimate=large,
        name="gather",
    )(feat.reshape(1), hits, *rows)


def combine_kernel(k_j, position_ref, rows_ref, out_ref):
    step = pl.program_id(0)
    s_dev = position_ref.shape[1]
    count = rows_ref.shape[0]
    here = lax.broadcasted_iota(jnp.int32, (s_dev, count), 1) + step * count
    rows = jnp.concatenate([position_ref[...], jnp.zeros((lane - 8, s_dev), f32)], axis=0)
    position = jnp.transpose(rows).astype(jnp.int32)
    hit = position[:, 0:1] == here
    for k in range(1, k_j):
        hit = jnp.logical_or(hit, position[:, k : k + 1] == here)
    part = jnp.dot(jnp.where(hit, 1.0, 0.0).astype(bf16), rows_ref[...], preferred_element_type=f32)

    @pl.when(step == 0)
    def _():
        out_ref[...] = part

    @pl.when(step > 0)
    def _():
        out_ref[...] += part


def combine(position, rows, k_j):
    s_dev = position.shape[1]
    total, width = rows.shape
    count = total // 6 if total % (6 * lane) == 0 else total
    return pl.pallas_call(
        functools.partial(combine_kernel, k_j),
        out_shape=jax.ShapeDtypeStruct((s_dev, width), f32),
        grid=(total // count,),
        in_specs=[
            pl.BlockSpec((8, s_dev), lambda i: (0, 0)),
            pl.BlockSpec((count, width), lambda i: (i, 0)),
        ],
        out_specs=pl.BlockSpec((s_dev, width), lambda i: (0, 0)),
        compiler_params=params(),
        name="combine",
    )(position, rows)


def block_pairs(width):
    n = width // lane
    return [(i, j) for i in range(n) for j in range(i, n)]


def gram_kernel(pairs_ref, sketch_ref, gram_ref):
    for at in range(gram_ref.shape[0]):
        left = sketch_ref[:, pl.ds(pl.multiple_of(pairs_ref[2 * at] * lane, lane), lane)]
        right = sketch_ref[:, pl.ds(pl.multiple_of(pairs_ref[2 * at + 1] * lane, lane), lane)]
        gram_ref[at] = lax.dot_general(left, right, COLS, preferred_element_type=f32).astype(bf16)


def gram_blocks(sketch, feat):
    width = sketch.shape[1]
    pairs = block_pairs(width)
    half = len(pairs) // 2
    table = jnp.asarray(np.array(pairs, np.int32).reshape(2, 2 * half))
    smem = pl.BlockSpec(memory_space=pltpu.SMEM)
    return pl.pallas_call(
        gram_kernel,
        out_shape=jax.ShapeDtypeStruct((half, lane, lane), bf16),
        in_specs=[smem, whole()],
        out_specs=whole(),
        compiler_params=params(),
        name="gram",
    )(table[feat % 2], sketch)


def halves(value):
    high = value.astype(bf16)
    return high, (value - high.astype(f32)).astype(bf16)


def dot(a, b):
    return jnp.dot(a, b, preferred_element_type=f32)


def dot3(a, b):
    (ah, al), (bh, bl) = halves(a), halves(b)
    return dot(jnp.concatenate([al, ah, ah], axis=1), jnp.concatenate([bh, bl, bh], axis=0))


def root_kernel(samples, place_ref, mine_gram_ref, other_gram_ref, mine_ref, out_ref, gram):
    width = mine_ref.shape[1]
    pairs = block_pairs(width)
    half = len(pairs) // 2
    odd = place_ref[0] % 2 == 1
    for at, (i, j) in enumerate(pairs):
        mine, other = mine_gram_ref[at % half].astype(f32), other_gram_ref[at % half].astype(f32)
        block = jnp.where(odd == (at < half), other, mine)
        gram[i * lane : (i + 1) * lane, j * lane : (j + 1) * lane] = block
        if i != j:
            gram[j * lane : (j + 1) * lane, i * lane : (i + 1) * lane] = jnp.transpose(block)
    rows = lax.broadcasted_iota(jnp.int32, (width, width), 0)
    ident = jnp.where(rows == lax.broadcasted_iota(jnp.int32, (width, width), 1), 1.0, 0.0)
    total = gram[...] + ridge * samples * ident
    scale = jnp.sum(total * ident, axis=(0, 1), keepdims=True) / width
    gap = 0.5 * ident - 0.5 * (total / scale)
    high, low = halves(gap)
    mine = mine_ref[...]
    value = mine.astype(f32) + dot(jnp.concatenate([mine, mine], axis=1), jnp.concatenate([low, high], axis=0))
    square = dot3(gap, gap)
    gap = 1.5 * square + dot3(square, gap)
    for _ in range(root_steps - 3):
        high = gap.astype(bf16)
        value = value + dot(value.astype(bf16), high)
        square = dot(high, high)
        gap = 1.5 * square + dot(square.astype(bf16), high)
    high = gap.astype(bf16)
    value = value + dot(value.astype(bf16), high)
    moved = dot(dot(value.astype(bf16), high).astype(bf16), high)
    value = value + 1.5 * moved + dot(moved.astype(bf16), high)
    out_ref[...] = (math.sqrt(samples) * lax.rsqrt(scale)) * value


def whiten(mine_gram, other_gram, mine, place, samples):
    width = mine.shape[1]
    return pl.pallas_call(
        functools.partial(root_kernel, samples),
        out_shape=jax.ShapeDtypeStruct(mine.shape, f32),
        in_specs=[pl.BlockSpec(memory_space=pltpu.SMEM), whole(), whole(), whole()],
        out_specs=whole(),
        scratch_shapes=[pltpu.VMEM((width, width), f32)],
        compiler_params=params(),
        name="root",
    )(place.reshape(1), mine_gram, other_gram, mine)


def crossed(value, axis, bits):
    count = lax.axis_size(axis)
    return lax.ppermute(value, axis, [(source, source ^ bits) for source in range(count)])


def total_of(values):
    total = values[0].astype(f32)
    for value in values[1:]:
        total = total + value.astype(f32)
    return total


def sum_over_dp(value):
    n_dp = lax.axis_size("dp")
    inner = math.gcd(n_dp, 4)
    me = lax.axis_index("dp") & (inner - 1)
    flat = value.reshape(-1, lane)
    rows = flat.shape[0] // inner
    parts = [lax.dynamic_slice_in_dim(flat, (me ^ bits) * rows, rows, 0) for bits in range(inner)]
    part = total_of([parts[0]] + [crossed(parts[bits], "dp", bits) for bits in range(1, inner)]).astype(bf16)
    if n_dp // inner == 4:
        part = total_of([part] + [crossed(part, "dp", bits * inner) for bits in range(1, 4)]).astype(bf16)
    else:
        bits = inner
        while bits < n_dp:
            part = total_of([part, crossed(part, "dp", bits)]).astype(bf16)
            bits *= 2
    pieces = jnp.stack([part] + [crossed(part, "dp", bits) for bits in range(1, inner)])
    return jnp.concatenate([pieces[me ^ at] for at in range(inner)], axis=0).reshape(value.shape)


def sketch_by_all_to_all(products, position, k_j):
    n_feat = lax.axis_size("feat")
    feat = lax.axis_index("feat")
    width = products.shape[2]
    returned = lax.all_to_all(products, "dp", split_axis=0, concat_axis=0, tiled=True)
    part = combine(position, returned.reshape(-1, width), k_j)
    bits = 1
    while bits < n_feat:
        part = part + crossed(part, "feat", bits)
        bits *= 2
    sketch = part.astype(bf16)
    own_rows = sketch.shape[0] // n_feat
    return lax.dynamic_slice_in_dim(sketch, feat * own_rows, own_rows, 0), sketch


def tied(value, *others):
    return lax.optimization_barrier((value, others))[0]


def sketch_by_planes(tiles, probe, position, inner, bound, k_j):
    n_dp, slots, _ = tiles.shape
    index, feat = lax.axis_index("dp"), lax.axis_index("feat")
    where = jnp.stack([index & (inner - 1), index // inner])
    positions = [position] + [crossed(position, "dp", c * inner) for c in range(1, n_dp // inner)]
    sent, hits = [], None
    for at, away in enumerate(stages):
        behind = positions if not at else sent[-1]
        if at == 2:
            hits = choose(where, tied(positions, sent[-1]), k_j, slots, inner)
            behind = hits
        sent.append(product(where, tied(tiles, behind), probe, inner, bound, away))
    plane, kept, behind = {}, [], None
    for at, away in enumerate(stages):
        rows = [sent[at][0]] + [crossed(sent[at][a], "dp", a) for a in range(1, inner)]
        if at:
            rows = tied(rows, kept[-1], (plane[3], sent[3]) if at == 2 else (plane[2], plane[1]) if at == 3 else kept[-1])
        keep, give = gather(feat, hits, rows, away)
        kept.append(keep)
        both = keep + crossed(give, "feat", 1).astype(f32)
        plane.update({c: both[i] for i, c in enumerate(away)})
        if at == 1:
            plane[2] = plane[2] + crossed(plane[3].astype(bf16), "dp", inner).astype(f32)
    plane[0] = plane[0] + crossed(plane[1].astype(bf16), "dp", inner).astype(f32)
    mine = (plane[0] + crossed(plane[2].astype(bf16), "dp", 2 * inner).astype(f32)).astype(bf16)
    return mine, jnp.concatenate([mine, crossed(mine, "feat", 1)], axis=0)


def local(grads, block_ids, probe):
    values = grads[0]
    s_dev, k_j, b_width = values.shape
    n_dp, n_feat = lax.axis_size("dp"), lax.axis_size("feat")
    feat = lax.axis_index("feat")
    per_dev = probe.shape[0]
    width = probe.shape[3]
    b_slice = per_dev * n_dp
    bound = max(2, 3 * s_dev * k_j // (2 * b_slice))
    probe = probe[:, 0]
    send, position = pack(block_ids[0].T, values.reshape(s_dev * k_j, b_width), n_dp, per_dev, bound)
    tiles = lax.all_to_all(send, "dp", split_axis=0, concat_axis=0, tiled=True)
    if n_feat == 2 and n_dp == 16:
        mine, sketch = sketch_by_planes(tiles, probe, position, 4, bound, k_j)
    else:
        products = product(jnp.zeros((2,), jnp.int32), tiles, probe, 1, bound, tuple(range(n_dp)))
        mine, sketch = sketch_by_all_to_all(products[0], position, k_j)
    mine_gram = sum_over_dp(gram_blocks(sketch, feat))
    other_gram = crossed(mine_gram, "feat", 1)
    return whiten(mine_gram, other_gram, mine, feat, s_dev * n_dp)


def solution(mesh):
    return jax.shard_map(
        local,
        mesh=mesh,
        in_specs=(P("feat", "dp", None, None), P("feat", "dp", None), P("dp", "feat", None, None)),
        out_specs=P(("dp", "feat"), None),
        check_vma=False,
    )
```

```python
import functools
import math

import jax
import jax.numpy as jnp
import numpy as np
from jax import lax
from jax.experimental import pallas as pl
from jax.experimental.pallas import tpu as pltpu
from jax.sharding import PartitionSpec as P

ridge = 0.1
root_steps = 4
f32 = jnp.float32
bf16 = jnp.bfloat16
lane = 128
stages = ((3,), (2,), (1,), (0,))

COLS = (((0,), (0,)), ((), ()))


large = pl.CostEstimate(flops=1 << 34, bytes_accessed=1, transcendentals=0)
small = pl.CostEstimate(flops=1, bytes_accessed=1, transcendentals=0)


def params(limit=24 << 20):
    return pltpu.CompilerParams(vmem_limit_bytes=limit)


def whole():
    return pl.BlockSpec(memory_space=pltpu.VMEM)


def joint_of(per_dev):
    return math.gcd(per_dev, 4)


def pack_kernel(per_dev, bound, ids_ref, values_ref, send_ref, position_ref, values, raw, arrived):
    k_j, s_dev = ids_ref.shape
    n_dp, slots, width = send_ref.shape
    n_ids = n_dp * per_dev
    joint = joint_of(per_dev)
    copy = pltpu.make_async_copy(values_ref, raw, arrived)
    copy.start()
    ids_rows = ids_ref[...]
    padded = jnp.concatenate([ids_rows.astype(f32), jnp.zeros((lane - k_j, s_dev), f32)], axis=0)
    ids_cols = jnp.transpose(padded)
    numbers = lax.broadcasted_iota(jnp.int32, (s_dev, n_ids), 1).astype(f32)
    number_rows = lax.broadcasted_iota(jnp.int32, (n_ids, s_dev), 0)
    earlier = (
        lax.broadcasted_iota(jnp.int32, (s_dev, s_dev), 0) > lax.broadcasted_iota(jnp.int32, (s_dev, s_dev), 1)
    )
    earlier = jnp.where(earlier, 1.0, 0.0).astype(bf16)
    used = jnp.zeros((1, n_ids), f32)
    places, by_rank, named_rows = [], [], []
    for k in range(k_j):
        column = ids_cols[:, k : k + 1]
        named = jnp.where(column == numbers, 1.0, 0.0)
        before = jnp.dot(earlier, named.astype(bf16), preferred_element_type=f32) + used
        rank = jnp.sum(named * before, axis=1, keepdims=True)
        used = used + jnp.sum(named, axis=0, keepdims=True)
        if k == 0:
            copy.wait()
            values[: raw.shape[0], :] = raw[...].astype(f32)
        tile = values[pl.ds(k, s_dev, stride=k_j), :]
        by_rank.append(jnp.concatenate([jnp.where(rank == r, tile, 0.0).astype(bf16) for r in range(bound)], axis=1))
        named_rows.append(jnp.where(ids_rows[k : k + 1, :] == number_rows, 1.0, 0.0).astype(bf16))
        id_col = column.astype(jnp.int32)
        group = id_col // joint
        places.append((group * bound + rank.astype(jnp.int32)) * joint + id_col - group * joint)
    named_rows, by_rank = jnp.concatenate(named_rows, axis=1), jnp.concatenate(by_rank, axis=0)
    total = jnp.dot(named_rows, by_rank, preferred_element_type=f32).astype(bf16)
    position = jnp.concatenate(places + [jnp.zeros((s_dev, lane - k_j), jnp.int32)], axis=1).astype(f32)
    position_ref[...] = jnp.transpose(position)[: position_ref.shape[0]]
    slot = lax.broadcasted_iota(jnp.int32, (slots, slots), 0)
    origin = lax.broadcasted_iota(jnp.int32, (slots, slots), 1)
    group = slot // (joint * bound)
    rank = (slot - group * (joint * bound)) // joint
    block = group * joint + slot % joint
    order = jnp.where(origin == rank * per_dev + block, 1.0, 0.0).astype(bf16)
    rows = [
        jnp.concatenate(
            [total[to * per_dev : (to + 1) * per_dev, r * width : (r + 1) * width] for r in range(bound)], axis=0
        )
        for to in range(n_dp)
    ]
    out = jnp.dot(order, jnp.concatenate(rows, axis=1), preferred_element_type=f32).astype(bf16)
    for to in range(n_dp):
        send_ref[to] = out[:, to * width : (to + 1) * width]


def pack(ids, values, n_dp, per_dev, bound):
    k_j, s_dev = ids.shape
    return pl.pallas_call(
        functools.partial(pack_kernel, per_dev, bound),
        out_shape=(
            jax.ShapeDtypeStruct((n_dp, bound * per_dev, lane), bf16),
            jax.ShapeDtypeStruct((8, s_dev), f32),
        ),
        in_specs=[whole(), pl.BlockSpec(memory_space=pl.ANY)],
        out_specs=(whole(), whole()),
        scratch_shapes=[
            pltpu.VMEM((values.shape[0] + 8, lane), f32),
            pltpu.VMEM(values.shape, bf16),
            pltpu.SemaphoreType.DMA,
        ],
        compiler_params=params(62 << 20),
        name="pack",
    )(ids, values)


def product_kernel(bound, joint, groups, away, where_ref, tiles_ref, probe_ref, *out_refs):
    inner = len(out_refs)
    width = out_refs[0].shape[2]
    count = inner * len(away)
    rows = bound * joint
    unit = groups * rows
    blocks = groups * joint
    units = probe_ref.shape[0] // blocks
    place, outer_at = where_ref[0], where_ref[1]
    own = lax.broadcasted_iota(jnp.int32, (count * rows, lane), 0) % joint
    for u in range(units):
        tiles = [
            tiles_ref[(outer_at ^ b) * inner + (place ^ a), u * unit : (u + 1) * unit, :].astype(f32)
            for a in range(inner)
            for b in away
        ]
        parts = []
        for g in range(groups):
            tile = jnp.concatenate([t[g * rows : (g + 1) * rows] for t in tiles], axis=0)
            spread = jnp.concatenate([jnp.where(own == j, tile, 0.0).astype(bf16) for j in range(joint)], axis=1)
            first = u * blocks + g * joint
            probe = probe_ref[first : first + joint].reshape(joint * lane, width)
            parts.append(jnp.dot(spread, probe, preferred_element_type=f32))
        for a in range(inner):
            for b in range(len(away)):
                at = (a * len(away) + b) * rows
                value = jnp.concatenate([part[at : at + rows] for part in parts], axis=0)
                out_refs[a][b, u * unit : (u + 1) * unit, :] = value.astype(bf16)


def product(where, tiles, probe, inner, bound, away):
    n_dp, slots, _ = tiles.shape
    per_dev, _, width = probe.shape
    joint = joint_of(per_dev)
    groups = 1 if bound * joint % 16 == 0 else 2
    return pl.pallas_call(
        functools.partial(product_kernel, bound, joint, groups, away),
        out_shape=[jax.ShapeDtypeStruct((len(away), slots, width), bf16)] * inner,
        in_specs=[pl.BlockSpec(memory_space=pltpu.SMEM), whole(), whole()],
        out_specs=[whole()] * inner,
        compiler_params=params(),
        cost_estimate=large,
        name="product",
    )(where, tiles, probe)


def choose_kernel(k_j, slots, inner, place_ref, *refs):
    position_refs, out_ref = refs[:-1], refs[-1]
    _, s_dev, count = out_ref.shape
    place, outer_at = place_ref[0], place_ref[1]
    at = lax.broadcasted_iota(jnp.int32, (1, count), 1)
    expect = jnp.zeros((1, count), jnp.int32)
    for a in range(inner):
        inside = jnp.logical_and(at >= a * slots, at < (a + 1) * slots)
        expect = jnp.where(inside, (outer_at * inner + (place ^ a)) * slots + at - a * slots, expect)
    expect = expect.astype(f32)
    rows = [ref[...] for ref in position_refs]
    rows = jnp.concatenate(rows + [jnp.zeros((lane - 8 * len(rows), s_dev), f32)], axis=0)
    columns = jnp.transpose(rows)
    for c in range(len(position_refs)):
        hit = columns[:, 8 * c : 8 * c + 1] == expect
        for k in range(1, k_j):
            hit = jnp.logical_or(hit, columns[:, 8 * c + k : 8 * c + k + 1] == expect)
        out_ref[c] = jnp.where(hit, 1.0, 0.0).astype(bf16)


def choose(where, positions, k_j, slots, inner):
    s_dev = positions[0].shape[1]
    return pl.pallas_call(
        functools.partial(choose_kernel, k_j, slots, inner),
        out_shape=jax.ShapeDtypeStruct((len(positions), s_dev, inner * slots), bf16),
        in_specs=[pl.BlockSpec(memory_space=pltpu.SMEM)] + [whole()] * len(positions),
        out_specs=whole(),
        compiler_params=params(),
        cost_estimate=large,
        name="choose",
    )(where, *positions)


def gather_kernel(away, feat_ref, hits_ref, *refs):
    rows_refs, (keep_ref, give_ref) = refs[:-2], refs[-2:]
    half = hits_ref.shape[1] // 2
    keep_at = pl.multiple_of(feat_ref[0] * half, half)
    give_at = pl.multiple_of((1 - feat_ref[0]) * half, half)
    for at, c in enumerate(away):
        rows = jnp.concatenate([ref[at] for ref in rows_refs], axis=0)
        give_ref[at] = jnp.dot(hits_ref[c, pl.ds(give_at, half), :], rows, preferred_element_type=f32).astype(bf16)
        keep_ref[at] = jnp.dot(hits_ref[c, pl.ds(keep_at, half), :], rows, preferred_element_type=f32)


def gather(feat, hits, rows, away):
    shape = (len(away), hits.shape[1] // 2, rows[0].shape[2])
    return pl.pallas_call(
        functools.partial(gather_kernel, away),
        out_shape=(jax.ShapeDtypeStruct(shape, f32), jax.ShapeDtypeStruct(shape, bf16)),
        in_specs=[pl.BlockSpec(memory_space=pltpu.SMEM)] + [whole()] * (1 + len(rows)),
        out_specs=(whole(), whole()),
        compiler_params=params(),
        cost_estimate=large,
        name="gather",
    )(feat.reshape(1), hits, *rows)


def combine_kernel(k_j, position_ref, rows_ref, out_ref):
    step = pl.program_id(0)
    s_dev = position_ref.shape[1]
    count = rows_ref.shape[0]
    here = lax.broadcasted_iota(jnp.int32, (s_dev, count), 1) + step * count
    rows = jnp.concatenate([position_ref[...], jnp.zeros((lane - 8, s_dev), f32)], axis=0)
    position = jnp.transpose(rows).astype(jnp.int32)
    hit = position[:, 0:1] == here
    for k in range(1, k_j):
        hit = jnp.logical_or(hit, position[:, k : k + 1] == here)
    part = jnp.dot(jnp.where(hit, 1.0, 0.0).astype(bf16), rows_ref[...], preferred_element_type=f32)

    @pl.when(step == 0)
    def _():
        out_ref[...] = part

    @pl.when(step > 0)
    def _():
        out_ref[...] += part


def combine(position, rows, k_j):
    s_dev = position.shape[1]
    total, width = rows.shape
    count = total // 6 if total % (6 * lane) == 0 else total
    return pl.pallas_call(
        functools.partial(combine_kernel, k_j),
        out_shape=jax.ShapeDtypeStruct((s_dev, width), f32),
        grid=(total // count,),
        in_specs=[
            pl.BlockSpec((8, s_dev), lambda i: (0, 0)),
            pl.BlockSpec((count, width), lambda i: (i, 0)),
        ],
        out_specs=pl.BlockSpec((s_dev, width), lambda i: (0, 0)),
        compiler_params=params(),
        name="combine",
    )(position, rows)


def block_pairs(width):
    n = width // lane
    return [(i, j) for i in range(n) for j in range(i, n)]


def gram_kernel(pairs_ref, sketch_ref, gram_ref):
    for at in range(gram_ref.shape[0]):
        left = sketch_ref[:, pl.ds(pl.multiple_of(pairs_ref[2 * at] * lane, lane), lane)]
        right = sketch_ref[:, pl.ds(pl.multiple_of(pairs_ref[2 * at + 1] * lane, lane), lane)]
        gram_ref[at] = lax.dot_general(left, right, COLS, preferred_element_type=f32).astype(bf16)


def gram_blocks(sketch, feat):
    width = sketch.shape[1]
    pairs = block_pairs(width)
    half = len(pairs) // 2
    table = jnp.asarray(np.array(pairs, np.int32).reshape(2, 2 * half))
    smem = pl.BlockSpec(memory_space=pltpu.SMEM)
    return pl.pallas_call(
        gram_kernel,
        out_shape=jax.ShapeDtypeStruct((half, lane, lane), bf16),
        in_specs=[smem, whole()],
        out_specs=whole(),
        compiler_params=params(),
        name="gram",
    )(table[feat % 2], sketch)


def halves(value):
    high = value.astype(bf16)
    return high, (value - high.astype(f32)).astype(bf16)


def dot(a, b):
    return jnp.dot(a, b, preferred_element_type=f32)


def dot3(a, b):
    (ah, al), (bh, bl) = halves(a), halves(b)
    return dot(jnp.concatenate([al, ah, ah], axis=1), jnp.concatenate([bh, bl, bh], axis=0))


def root_kernel(samples, place_ref, mine_gram_ref, other_gram_ref, mine_ref, out_ref, gram):
    width = mine_ref.shape[1]
    pairs = block_pairs(width)
    half = len(pairs) // 2
    odd = place_ref[0] % 2 == 1
    for at, (i, j) in enumerate(pairs):
        mine, other = mine_gram_ref[at % half].astype(f32), other_gram_ref[at % half].astype(f32)
        block = jnp.where(odd == (at < half), other, mine)
        gram[i * lane : (i + 1) * lane, j * lane : (j + 1) * lane] = block
        if i != j:
            gram[j * lane : (j + 1) * lane, i * lane : (i + 1) * lane] = jnp.transpose(block)
    rows = lax.broadcasted_iota(jnp.int32, (width, width), 0)
    ident = jnp.where(rows == lax.broadcasted_iota(jnp.int32, (width, width), 1), 1.0, 0.0)
    total = gram[...] + ridge * samples * ident
    scale = jnp.sum(total * ident, axis=(0, 1), keepdims=True) / width
    gap = 0.5 * ident - 0.5 * (total / scale)
    high, low = halves(gap)
    mine = mine_ref[...]
    value = mine.astype(f32) + dot(jnp.concatenate([mine, mine], axis=1), jnp.concatenate([low, high], axis=0))
    square = dot3(gap, gap)
    gap = 1.5 * square + dot3(square, gap)
    for _ in range(root_steps - 3):
        high = gap.astype(bf16)
        value = value + dot(value.astype(bf16), high)
        square = dot(high, high)
        gap = 1.5 * square + dot(square.astype(bf16), high)
    high = gap.astype(bf16)
    value = value + dot(value.astype(bf16), high)
    moved = dot(dot(value.astype(bf16), high).astype(bf16), high)
    value = value + 1.5 * moved + dot(moved.astype(bf16), high)
    out_ref[...] = (math.sqrt(samples) * lax.rsqrt(scale)) * value


def whiten(mine_gram, other_gram, mine, place, samples):
    width = mine.shape[1]
    return pl.pallas_call(
        functools.partial(root_kernel, samples),
        out_shape=jax.ShapeDtypeStruct(mine.shape, f32),
        in_specs=[pl.BlockSpec(memory_space=pltpu.SMEM), whole(), whole(), whole()],
        out_specs=whole(),
        scratch_shapes=[pltpu.VMEM((width, width), f32)],
        compiler_params=params(),
        name="root",
    )(place.reshape(1), mine_gram, other_gram, mine)


def crossed(value, axis, bits):
    count = lax.axis_size(axis)
    return lax.ppermute(value, axis, [(source, source ^ bits) for source in range(count)])


def total_of(values):
    total = values[0].astype(f32)
    for value in values[1:]:
        total = total + value.astype(f32)
    return total


def sum_over_dp(value):
    n_dp = lax.axis_size("dp")
    inner = math.gcd(n_dp, 4)
    me = lax.axis_index("dp") & (inner - 1)
    flat = value.reshape(-1, lane)
    rows = flat.shape[0] // inner
    parts = [lax.dynamic_slice_in_dim(flat, (me ^ bits) * rows, rows, 0) for bits in range(inner)]
    part = total_of([parts[0]] + [crossed(parts[bits], "dp", bits) for bits in range(1, inner)]).astype(bf16)
    if n_dp // inner == 4:
        part = total_of([part] + [crossed(part, "dp", bits * inner) for bits in range(1, 4)]).astype(bf16)
    else:
        bits = inner
        while bits < n_dp:
            part = total_of([part, crossed(part, "dp", bits)]).astype(bf16)
            bits *= 2
    pieces = jnp.stack([part] + [crossed(part, "dp", bits) for bits in range(1, inner)])
    return jnp.concatenate([pieces[me ^ at] for at in range(inner)], axis=0).reshape(value.shape)


def sketch_by_all_to_all(products, position, k_j):
    n_feat = lax.axis_size("feat")
    feat = lax.axis_index("feat")
    width = products.shape[2]
    returned = lax.all_to_all(products, "dp", split_axis=0, concat_axis=0, tiled=True)
    part = combine(position, returned.reshape(-1, width), k_j)
    bits = 1
    while bits < n_feat:
        part = part + crossed(part, "feat", bits)
        bits *= 2
    sketch = part.astype(bf16)
    own_rows = sketch.shape[0] // n_feat
    return lax.dynamic_slice_in_dim(sketch, feat * own_rows, own_rows, 0), sketch


def tied(value, *others):
    return lax.optimization_barrier((value, others))[0]


def sketch_by_planes(tiles, probe, position, inner, bound, k_j):
    n_dp, slots, _ = tiles.shape
    index, feat = lax.axis_index("dp"), lax.axis_index("feat")
    where = jnp.stack([index & (inner - 1), index // inner])
    positions = [position] + [crossed(position, "dp", c * inner) for c in range(1, n_dp // inner)]
    sent, hits = [], None
    for at, away in enumerate(stages):
        behind = positions if not at else sent[-1]
        if at == 2:
            hits = choose(where, tied(positions, sent[-1]), k_j, slots, inner)
            behind = hits
        sent.append(product(where, tied(tiles, behind), probe, inner, bound, away))
    plane, kept, behind = {}, [], None
    for at, away in enumerate(stages):
        rows = [sent[at][0]] + [crossed(sent[at][a], "dp", a) for a in range(1, inner)]
        if at:
            rows = tied(rows, kept[-1], (plane[3], sent[3]) if at == 2 else (plane[2], plane[1]) if at == 3 else kept[-1])
        keep, give = gather(feat, hits, rows, away)
        kept.append(keep)
        both = keep + crossed(give, "feat", 1).astype(f32)
        plane.update({c: both[i] for i, c in enumerate(away)})
        if at == 1:
            plane[2] = plane[2] + crossed(plane[3].astype(bf16), "dp", inner).astype(f32)
    plane[0] = plane[0] + crossed(plane[1].astype(bf16), "dp", inner).astype(f32)
    mine = (plane[0] + crossed(plane[2].astype(bf16), "dp", 2 * inner).astype(f32)).astype(bf16)
    return mine, jnp.concatenate([mine, crossed(mine, "feat", 1)], axis=0)


def local(grads, block_ids, probe):
    values = grads[0]
    s_dev, k_j, b_width = values.shape
    n_dp, n_feat = lax.axis_size("dp"), lax.axis_size("feat")
    feat = lax.axis_index("feat")
    per_dev = probe.shape[0]
    width = probe.shape[3]
    b_slice = per_dev * n_dp
    bound = max(2, 3 * s_dev * k_j // (2 * b_slice))
    probe = probe[:, 0]
    send, position = pack(block_ids[0].T, values.reshape(s_dev * k_j, b_width), n_dp, per_dev, bound)
    tiles = lax.all_to_all(send, "dp", split_axis=0, concat_axis=0, tiled=True)
    if n_feat == 2 and n_dp == 16:
        mine, sketch = sketch_by_planes(tiles, probe, position, 4, bound, k_j)
    else:
        products = product(jnp.zeros((2,), jnp.int32), tiles, probe, 1, bound, tuple(range(n_dp)))
        mine, sketch = sketch_by_all_to_all(products[0], position, k_j)
    mine_gram = sum_over_dp(gram_blocks(sketch, feat))
    other_gram = crossed(mine_gram, "feat", 1)
    return whiten(mine_gram, other_gram, mine, feat, s_dev * n_dp)


def solution(mesh):
    return jax.shard_map(
        local,
        mesh=mesh,
        in_specs=(P("feat", "dp", None, None), P("feat", "dp", None), P("dp", "feat", None, None)),
        out_specs=P(("dp", "feat"), None),
        check_vma=False,
    )
```

```python
import functools
import math

import jax
import jax.numpy as jnp
import numpy as np
from jax import lax
from jax.experimental import pallas as pl
from jax.experimental.pallas import tpu as pltpu
from jax.sharding import PartitionSpec as P

ridge = 0.1
root_steps = 4
f32 = jnp.float32
bf16 = jnp.bfloat16
lane = 128
stages = ((3,), (2,), (1,), (0,))

COLS = (((0,), (0,)), ((), ()))


large = pl.CostEstimate(flops=1 << 34, bytes_accessed=1, transcendentals=0)
small = pl.CostEstimate(flops=1, bytes_accessed=1, transcendentals=0)


def params(limit=24 << 20):
    return pltpu.CompilerParams(vmem_limit_bytes=limit)


def whole():
    return pl.BlockSpec(memory_space=pltpu.VMEM)


def joint_of(per_dev):
    return math.gcd(per_dev, 4)


def pack_kernel(per_dev, bound, ids_ref, values_ref, send_ref, position_ref, values, raw, arrived):
    k_j, s_dev = ids_ref.shape
    n_dp, slots, width = send_ref.shape
    n_ids = n_dp * per_dev
    joint = joint_of(per_dev)
    copy = pltpu.make_async_copy(values_ref, raw, arrived)
    copy.start()
    ids_rows = ids_ref[...]
    padded = jnp.concatenate([ids_rows.astype(f32), jnp.zeros((lane - k_j, s_dev), f32)], axis=0)
    ids_cols = jnp.transpose(padded)
    numbers = lax.broadcasted_iota(jnp.int32, (s_dev, n_ids), 1).astype(f32)
    number_rows = lax.broadcasted_iota(jnp.int32, (n_ids, s_dev), 0)
    earlier = (
        lax.broadcasted_iota(jnp.int32, (s_dev, s_dev), 0) > lax.broadcasted_iota(jnp.int32, (s_dev, s_dev), 1)
    )
    earlier = jnp.where(earlier, 1.0, 0.0).astype(bf16)
    used = jnp.zeros((1, n_ids), f32)
    places, by_rank, named_rows = [], [], []
    for k in range(k_j):
        column = ids_cols[:, k : k + 1]
        named = jnp.where(column == numbers, 1.0, 0.0)
        before = jnp.dot(earlier, named.astype(bf16), preferred_element_type=f32) + used
        rank = jnp.sum(named * before, axis=1, keepdims=True)
        used = used + jnp.sum(named, axis=0, keepdims=True)
        if k == 0:
            copy.wait()
            values[: raw.shape[0], :] = raw[...].astype(f32)
        tile = values[pl.ds(k, s_dev, stride=k_j), :]
        by_rank.append(jnp.concatenate([jnp.where(rank == r, tile, 0.0).astype(bf16) for r in range(bound)], axis=1))
        named_rows.append(jnp.where(ids_rows[k : k + 1, :] == number_rows, 1.0, 0.0).astype(bf16))
        id_col = column.astype(jnp.int32)
        group = id_col // joint
        places.append((group * bound + rank.astype(jnp.int32)) * joint + id_col - group * joint)
    named_rows, by_rank = jnp.concatenate(named_rows, axis=1), jnp.concatenate(by_rank, axis=0)
    total = jnp.dot(named_rows, by_rank, preferred_element_type=f32).astype(bf16)
    position = jnp.concatenate(places + [jnp.zeros((s_dev, lane - k_j), jnp.int32)], axis=1).astype(f32)
    position_ref[...] = jnp.transpose(position)[: position_ref.shape[0]]
    slot = lax.broadcasted_iota(jnp.int32, (slots, slots), 0)
    origin = lax.broadcasted_iota(jnp.int32, (slots, slots), 1)
    group = slot // (joint * bound)
    rank = (slot - group * (joint * bound)) // joint
    block = group * joint + slot % joint
    order = jnp.where(origin == rank * per_dev + block, 1.0, 0.0).astype(bf16)
    rows = [
        jnp.concatenate(
            [total[to * per_dev : (to + 1) * per_dev, r * width : (r + 1) * width] for r in range(bound)], axis=0
        )
        for to in range(n_dp)
    ]
    out = jnp.dot(order, jnp.concatenate(rows, axis=1), preferred_element_type=f32).astype(bf16)
    for to in range(n_dp):
        send_ref[to] = out[:, to * width : (to + 1) * width]


def pack(ids, values, n_dp, per_dev, bound):
    k_j, s_dev = ids.shape
    return pl.pallas_call(
        functools.partial(pack_kernel, per_dev, bound),
        out_shape=(
            jax.ShapeDtypeStruct((n_dp, bound * per_dev, lane), bf16),
            jax.ShapeDtypeStruct((8, s_dev), f32),
        ),
        in_specs=[whole(), pl.BlockSpec(memory_space=pl.ANY)],
        out_specs=(whole(), whole()),
        scratch_shapes=[
            pltpu.VMEM((values.shape[0] + 8, lane), f32),
            pltpu.VMEM(values.shape, bf16),
            pltpu.SemaphoreType.DMA,
        ],
        compiler_params=params(62 << 20),
        name="pack",
    )(ids, values)


def product_kernel(bound, joint, groups, away, where_ref, tiles_ref, probe_ref, *out_refs):
    inner = len(out_refs)
    width = out_refs[0].shape[2]
    count = inner * len(away)
    rows = bound * joint
    unit = groups * rows
    blocks = groups * joint
    units = probe_ref.shape[0] // blocks
    place, outer_at = where_ref[0], where_ref[1]
    own = lax.broadcasted_iota(jnp.int32, (count * rows, lane), 0) % joint
    for u in range(units):
        tiles = [
            tiles_ref[(outer_at ^ b) * inner + (place ^ a), u * unit : (u + 1) * unit, :].astype(f32)
            for a in range(inner)
            for b in away
        ]
        parts = []
        for g in range(groups):
            tile = jnp.concatenate([t[g * rows : (g + 1) * rows] for t in tiles], axis=0)
            spread = jnp.concatenate([jnp.where(own == j, tile, 0.0).astype(bf16) for j in range(joint)], axis=1)
            first = u * blocks + g * joint
            probe = probe_ref[first : first + joint].reshape(joint * lane, width)
            parts.append(jnp.dot(spread, probe, preferred_element_type=f32))
        for a in range(inner):
            for b in range(len(away)):
                at = (a * len(away) + b) * rows
                value = jnp.concatenate([part[at : at + rows] for part in parts], axis=0)
                out_refs[a][b, u * unit : (u + 1) * unit, :] = value.astype(bf16)


def product(where, tiles, probe, inner, bound, away):
    n_dp, slots, _ = tiles.shape
    per_dev, _, width = probe.shape
    joint = joint_of(per_dev)
    groups = 1 if bound * joint % 16 == 0 else 2
    return pl.pallas_call(
        functools.partial(product_kernel, bound, joint, groups, away),
        out_shape=[jax.ShapeDtypeStruct((len(away), slots, width), bf16)] * inner,
        in_specs=[pl.BlockSpec(memory_space=pltpu.SMEM), whole(), whole()],
        out_specs=[whole()] * inner,
        compiler_params=params(),
        cost_estimate=large,
        name="product",
    )(where, tiles, probe)


def choose_kernel(k_j, slots, inner, place_ref, *refs):
    position_refs, out_ref = refs[:-1], refs[-1]
    _, s_dev, count = out_ref.shape
    place, outer_at = place_ref[0], place_ref[1]
    at = lax.broadcasted_iota(jnp.int32, (1, count), 1)
    expect = jnp.zeros((1, count), jnp.int32)
    for a in range(inner):
        inside = jnp.logical_and(at >= a * slots, at < (a + 1) * slots)
        expect = jnp.where(inside, (outer_at * inner + (place ^ a)) * slots + at - a * slots, expect)
    expect = expect.astype(f32)
    rows = [ref[...] for ref in position_refs]
    rows = jnp.concatenate(rows + [jnp.zeros((lane - 8 * len(rows), s_dev), f32)], axis=0)
    columns = jnp.transpose(rows)
    for c in range(len(position_refs)):
        hit = columns[:, 8 * c : 8 * c + 1] == expect
        for k in range(1, k_j):
            hit = jnp.logical_or(hit, columns[:, 8 * c + k : 8 * c + k + 1] == expect)
        out_ref[c] = jnp.where(hit, 1.0, 0.0).astype(bf16)


def choose(where, positions, k_j, slots, inner):
    s_dev = positions[0].shape[1]
    return pl.pallas_call(
        functools.partial(choose_kernel, k_j, slots, inner),
        out_shape=jax.ShapeDtypeStruct((len(positions), s_dev, inner * slots), bf16),
        in_specs=[pl.BlockSpec(memory_space=pltpu.SMEM)] + [whole()] * len(positions),
        out_specs=whole(),
        compiler_params=params(),
        cost_estimate=large,
        name="choose",
    )(where, *positions)


def gather_kernel(away, feat_ref, hits_ref, *refs):
    rows_refs, (keep_ref, give_ref) = refs[:-2], refs[-2:]
    half = hits_ref.shape[1] // 2
    keep_at = pl.multiple_of(feat_ref[0] * half, half)
    give_at = pl.multiple_of((1 - feat_ref[0]) * half, half)
    for at, c in enumerate(away):
        rows = jnp.concatenate([ref[at] for ref in rows_refs], axis=0)
        give_ref[at] = jnp.dot(hits_ref[c, pl.ds(give_at, half), :], rows, preferred_element_type=f32).astype(bf16)
        keep_ref[at] = jnp.dot(hits_ref[c, pl.ds(keep_at, half), :], rows, preferred_element_type=f32)


def gather(feat, hits, rows, away):
    shape = (len(away), hits.shape[1] // 2, rows[0].shape[2])
    return pl.pallas_call(
        functools.partial(gather_kernel, away),
        out_shape=(jax.ShapeDtypeStruct(shape, f32), jax.ShapeDtypeStruct(shape, bf16)),
        in_specs=[pl.BlockSpec(memory_space=pltpu.SMEM)] + [whole()] * (1 + len(rows)),
        out_specs=(whole(), whole()),
        compiler_params=params(),
        cost_estimate=large,
        name="gather",
    )(feat.reshape(1), hits, *rows)


def combine_kernel(k_j, position_ref, rows_ref, out_ref):
    step = pl.program_id(0)
    s_dev = position_ref.shape[1]
    count = rows_ref.shape[0]
    here = lax.broadcasted_iota(jnp.int32, (s_dev, count), 1) + step * count
    rows = jnp.concatenate([position_ref[...], jnp.zeros((lane - 8, s_dev), f32)], axis=0)
    position = jnp.transpose(rows).astype(jnp.int32)
    hit = position[:, 0:1] == here
    for k in range(1, k_j):
        hit = jnp.logical_or(hit, position[:, k : k + 1] == here)
    part = jnp.dot(jnp.where(hit, 1.0, 0.0).astype(bf16), rows_ref[...], preferred_element_type=f32)

    @pl.when(step == 0)
    def _():
        out_ref[...] = part

    @pl.when(step > 0)
    def _():
        out_ref[...] += part


def combine(position, rows, k_j):
    s_dev = position.shape[1]
    total, width = rows.shape
    count = total // 6 if total % (6 * lane) == 0 else total
    return pl.pallas_call(
        functools.partial(combine_kernel, k_j),
        out_shape=jax.ShapeDtypeStruct((s_dev, width), f32),
        grid=(total // count,),
        in_specs=[
            pl.BlockSpec((8, s_dev), lambda i: (0, 0)),
            pl.BlockSpec((count, width), lambda i: (i, 0)),
        ],
        out_specs=pl.BlockSpec((s_dev, width), lambda i: (0, 0)),
        compiler_params=params(),
        name="combine",
    )(position, rows)


def block_pairs(width):
    n = width // lane
    return [(i, j) for i in range(n) for j in range(i, n)]


def gram_kernel(pairs_ref, sketch_ref, gram_ref):
    for at in range(gram_ref.shape[0]):
        left = sketch_ref[:, pl.ds(pl.multiple_of(pairs_ref[2 * at] * lane, lane), lane)]
        right = sketch_ref[:, pl.ds(pl.multiple_of(pairs_ref[2 * at + 1] * lane, lane), lane)]
        gram_ref[at] = lax.dot_general(left, right, COLS, preferred_element_type=f32).astype(bf16)


def gram_blocks(sketch, feat):
    width = sketch.shape[1]
    pairs = block_pairs(width)
    half = len(pairs) // 2
    table = jnp.asarray(np.array(pairs, np.int32).reshape(2, 2 * half))
    smem = pl.BlockSpec(memory_space=pltpu.SMEM)
    return pl.pallas_call(
        gram_kernel,
        out_shape=jax.ShapeDtypeStruct((half, lane, lane), bf16),
        in_specs=[smem, whole()],
        out_specs=whole(),
        compiler_params=params(),
        name="gram",
    )(table[feat % 2], sketch)


def halves(value):
    high = value.astype(bf16)
    return high, (value - high.astype(f32)).astype(bf16)


def dot(a, b):
    return jnp.dot(a, b, preferred_element_type=f32)


def dot3(a, b):
    (ah, al), (bh, bl) = halves(a), halves(b)
    return dot(jnp.concatenate([al, ah, ah], axis=1), jnp.concatenate([bh, bl, bh], axis=0))


def root_kernel(samples, place_ref, mine_gram_ref, other_gram_ref, mine_ref, out_ref, gram):
    width = mine_ref.shape[1]
    pairs = block_pairs(width)
    half = len(pairs) // 2
    odd = place_ref[0] % 2 == 1
    for at, (i, j) in enumerate(pairs):
        mine, other = mine_gram_ref[at % half].astype(f32), other_gram_ref[at % half].astype(f32)
        block = jnp.where(odd == (at < half), other, mine)
        gram[i * lane : (i + 1) * lane, j * lane : (j + 1) * lane] = block
        if i != j:
            gram[j * lane : (j + 1) * lane, i * lane : (i + 1) * lane] = jnp.transpose(block)
    rows = lax.broadcasted_iota(jnp.int32, (width, width), 0)
    ident = jnp.where(rows == lax.broadcasted_iota(jnp.int32, (width, width), 1), 1.0, 0.0)
    total = gram[...] + ridge * samples * ident
    scale = jnp.sum(total * ident, axis=(0, 1), keepdims=True) / width
    gap = 0.5 * ident - 0.5 * (total / scale)
    high, low = halves(gap)
    mine = mine_ref[...]
    value = mine.astype(f32) + dot(jnp.concatenate([mine, mine], axis=1), jnp.concatenate([low, high], axis=0))
    square = dot3(gap, gap)
    gap = 1.5 * square + dot3(square, gap)
    for _ in range(root_steps - 3):
        high = gap.astype(bf16)
        value = value + dot(value.astype(bf16), high)
        square = dot(high, high)
        gap = 1.5 * square + dot(square.astype(bf16), high)
    high = gap.astype(bf16)
    value = value + dot(value.astype(bf16), high)
    moved = dot(dot(value.astype(bf16), high).astype(bf16), high)
    value = value + 1.5 * moved + dot(moved.astype(bf16), high)
    out_ref[...] = (math.sqrt(samples) * lax.rsqrt(scale)) * value


def whiten(mine_gram, other_gram, mine, place, samples):
    width = mine.shape[1]
    return pl.pallas_call(
        functools.partial(root_kernel, samples),
        out_shape=jax.ShapeDtypeStruct(mine.shape, f32),
        in_specs=[pl.BlockSpec(memory_space=pltpu.SMEM), whole(), whole(), whole()],
        out_specs=whole(),
        scratch_shapes=[pltpu.VMEM((width, width), f32)],
        compiler_params=params(),
        name="root",
    )(place.reshape(1), mine_gram, other_gram, mine)


def crossed(value, axis, bits):
    count = lax.axis_size(axis)
    return lax.ppermute(value, axis, [(source, source ^ bits) for source in range(count)])


def total_of(values):
    total = values[0].astype(f32)
    for value in values[1:]:
        total = total + value.astype(f32)
    return total


def sum_over_dp(value):
    n_dp = lax.axis_size("dp")
    inner = math.gcd(n_dp, 4)
    me = lax.axis_index("dp") & (inner - 1)
    flat = value.reshape(-1, lane)
    rows = flat.shape[0] // inner
    parts = [lax.dynamic_slice_in_dim(flat, (me ^ bits) * rows, rows, 0) for bits in range(inner)]
    part = total_of([parts[0]] + [crossed(parts[bits], "dp", bits) for bits in range(1, inner)]).astype(bf16)
    if n_dp // inner == 4:
        part = total_of([part] + [crossed(part, "dp", bits * inner) for bits in range(1, 4)]).astype(bf16)
    else:
        bits = inner
        while bits < n_dp:
            part = total_of([part, crossed(part, "dp", bits)]).astype(bf16)
            bits *= 2
    pieces = jnp.stack([part] + [crossed(part, "dp", bits) for bits in range(1, inner)])
    return jnp.concatenate([pieces[me ^ at] for at in range(inner)], axis=0).reshape(value.shape)


def sketch_by_all_to_all(products, position, k_j):
    n_feat = lax.axis_size("feat")
    feat = lax.axis_index("feat")
    width = products.shape[2]
    returned = lax.all_to_all(products, "dp", split_axis=0, concat_axis=0, tiled=True)
    part = combine(position, returned.reshape(-1, width), k_j)
    bits = 1
    while bits < n_feat:
        part = part + crossed(part, "feat", bits)
        bits *= 2
    sketch = part.astype(bf16)
    own_rows = sketch.shape[0] // n_feat
    return lax.dynamic_slice_in_dim(sketch, feat * own_rows, own_rows, 0), sketch


def tied(value, *others):
    return lax.optimization_barrier((value, others))[0]


def sketch_by_planes(tiles, probe, position, inner, bound, k_j):
    n_dp, slots, _ = tiles.shape
    index, feat = lax.axis_index("dp"), lax.axis_index("feat")
    where = jnp.stack([index & (inner - 1), index // inner])
    positions = [position] + [crossed(position, "dp", c * inner) for c in range(1, n_dp // inner)]
    sent, hits = [], None
    for at, away in enumerate(stages[:3]):
        behind = positions if not at else sent[-1]
        if at == 2:
            hits = choose(where, tied(positions, sent[-1]), k_j, slots, inner)
            behind = hits
        sent.append(product(where, tied(tiles, behind), probe, inner, bound, away))
    plane, kept, behind = {}, [], None
    for at, away in enumerate(stages):
        if at == 1:
            sent.append(product(where, tied(tiles, kept[0]), probe, inner, bound, stages[3]))
        rows = [sent[at][0]] + [crossed(sent[at][a], "dp", a) for a in range(1, inner)]
        if at:
            rows = tied(rows, kept[-1], (plane[3], sent[3]) if at == 2 else (plane[2], plane[1]) if at == 3 else sent[3])
        keep, give = gather(feat, hits, rows, away)
        kept.append(keep)
        both = keep + crossed(give, "feat", 1).astype(f32)
        plane.update({c: both[i] for i, c in enumerate(away)})
        if at == 1:
            plane[2] = plane[2] + crossed(plane[3].astype(bf16), "dp", inner).astype(f32)
    plane[0] = plane[0] + crossed(plane[1].astype(bf16), "dp", inner).astype(f32)
    mine = (plane[0] + crossed(plane[2].astype(bf16), "dp", 2 * inner).astype(f32)).astype(bf16)
    return mine, jnp.concatenate([mine, crossed(mine, "feat", 1)], axis=0)


def local(grads, block_ids, probe):
    values = grads[0]
    s_dev, k_j, b_width = values.shape
    n_dp, n_feat = lax.axis_size("dp"), lax.axis_size("feat")
    feat = lax.axis_index("feat")
    per_dev = probe.shape[0]
    width = probe.shape[3]
    b_slice = per_dev * n_dp
    bound = max(2, 3 * s_dev * k_j // (2 * b_slice))
    probe = probe[:, 0]
    send, position = pack(block_ids[0].T, values.reshape(s_dev * k_j, b_width), n_dp, per_dev, bound)
    tiles = lax.all_to_all(send, "dp", split_axis=0, concat_axis=0, tiled=True)
    if n_feat == 2 and n_dp == 16:
        mine, sketch = sketch_by_planes(tiles, probe, position, 4, bound, k_j)
    else:
        products = product(jnp.zeros((2,), jnp.int32), tiles, probe, 1, bound, tuple(range(n_dp)))
        mine, sketch = sketch_by_all_to_all(products[0], position, k_j)
    mine_gram = sum_over_dp(gram_blocks(sketch, feat))
    other_gram = crossed(mine_gram, "feat", 1)
    return whiten(mine_gram, other_gram, mine, feat, s_dev * n_dp)


def solution(mesh):
    return jax.shard_map(
        local,
        mesh=mesh,
        in_specs=(P("feat", "dp", None, None), P("feat", "dp", None), P("dp", "feat", None, None)),
        out_specs=P(("dp", "feat"), None),
        check_vma=False,
    )
```

```python
import functools
import math

import jax
import jax.numpy as jnp
import numpy as np
from jax import lax
from jax.experimental import pallas as pl
from jax.experimental.pallas import tpu as pltpu
from jax.sharding import PartitionSpec as P

ridge = 0.1
root_steps = 4
f32 = jnp.float32
bf16 = jnp.bfloat16
lane = 128
stages = ((3,), (2,), (1,), (0,))

COLS = (((0,), (0,)), ((), ()))


large = pl.CostEstimate(flops=1 << 34, bytes_accessed=1, transcendentals=0)
small = pl.CostEstimate(flops=1, bytes_accessed=1, transcendentals=0)


def params(limit=24 << 20):
    return pltpu.CompilerParams(vmem_limit_bytes=limit)


def whole():
    return pl.BlockSpec(memory_space=pltpu.VMEM)


def joint_of(per_dev):
    return math.gcd(per_dev, 4)


def pack_kernel(per_dev, bound, ids_ref, values_ref, send_ref, position_ref, values, raw, arrived):
    k_j, s_dev = ids_ref.shape
    n_dp, slots, width = send_ref.shape
    n_ids = n_dp * per_dev
    joint = joint_of(per_dev)
    copy = pltpu.make_async_copy(values_ref, raw, arrived)
    copy.start()
    ids_rows = ids_ref[...]
    padded = jnp.concatenate([ids_rows.astype(f32), jnp.zeros((lane - k_j, s_dev), f32)], axis=0)
    ids_cols = jnp.transpose(padded)
    numbers = lax.broadcasted_iota(jnp.int32, (s_dev, n_ids), 1).astype(f32)
    number_rows = lax.broadcasted_iota(jnp.int32, (n_ids, s_dev), 0)
    earlier = (
        lax.broadcasted_iota(jnp.int32, (s_dev, s_dev), 0) > lax.broadcasted_iota(jnp.int32, (s_dev, s_dev), 1)
    )
    earlier = jnp.where(earlier, 1.0, 0.0).astype(bf16)
    used = jnp.zeros((1, n_ids), f32)
    places, by_rank, named_rows = [], [], []
    for k in range(k_j):
        column = ids_cols[:, k : k + 1]
        named = jnp.where(column == numbers, 1.0, 0.0)
        before = jnp.dot(earlier, named.astype(bf16), preferred_element_type=f32) + used
        rank = jnp.sum(named * before, axis=1, keepdims=True)
        used = used + jnp.sum(named, axis=0, keepdims=True)
        if k == 0:
            copy.wait()
            values[: raw.shape[0], :] = raw[...].astype(f32)
        tile = values[pl.ds(k, s_dev, stride=k_j), :]
        by_rank.append(jnp.concatenate([jnp.where(rank == r, tile, 0.0).astype(bf16) for r in range(bound)], axis=1))
        named_rows.append(jnp.where(ids_rows[k : k + 1, :] == number_rows, 1.0, 0.0).astype(bf16))
        id_col = column.astype(jnp.int32)
        group = id_col // joint
        places.append((group * bound + rank.astype(jnp.int32)) * joint + id_col - group * joint)
    named_rows, by_rank = jnp.concatenate(named_rows, axis=1), jnp.concatenate(by_rank, axis=0)
    total = jnp.dot(named_rows, by_rank, preferred_element_type=f32).astype(bf16)
    position = jnp.concatenate(places + [jnp.zeros((s_dev, lane - k_j), jnp.int32)], axis=1).astype(f32)
    position_ref[...] = jnp.transpose(position)[: position_ref.shape[0]]
    slot = lax.broadcasted_iota(jnp.int32, (slots, slots), 0)
    origin = lax.broadcasted_iota(jnp.int32, (slots, slots), 1)
    group = slot // (joint * bound)
    rank = (slot - group * (joint * bound)) // joint
    block = group * joint + slot % joint
    order = jnp.where(origin == rank * per_dev + block, 1.0, 0.0).astype(bf16)
    rows = [
        jnp.concatenate(
            [total[to * per_dev : (to + 1) * per_dev, r * width : (r + 1) * width] for r in range(bound)], axis=0
        )
        for to in range(n_dp)
    ]
    out = jnp.dot(order, jnp.concatenate(rows, axis=1), preferred_element_type=f32).astype(bf16)
    for to in range(n_dp):
        send_ref[to] = out[:, to * width : (to + 1) * width]


def pack(ids, values, n_dp, per_dev, bound):
    k_j, s_dev = ids.shape
    return pl.pallas_call(
        functools.partial(pack_kernel, per_dev, bound),
        out_shape=(
            jax.ShapeDtypeStruct((n_dp, bound * per_dev, lane), bf16),
            jax.ShapeDtypeStruct((8, s_dev), f32),
        ),
        in_specs=[whole(), pl.BlockSpec(memory_space=pl.ANY)],
        out_specs=(whole(), whole()),
        scratch_shapes=[
            pltpu.VMEM((values.shape[0] + 8, lane), f32),
            pltpu.VMEM(values.shape, bf16),
            pltpu.SemaphoreType.DMA,
        ],
        compiler_params=params(62 << 20),
        name="pack",
    )(ids, values)


def product_kernel(bound, joint, groups, away, where_ref, tiles_ref, probe_ref, *out_refs):
    inner = len(out_refs)
    width = out_refs[0].shape[2]
    count = inner * len(away)
    rows = bound * joint
    unit = groups * rows
    blocks = groups * joint
    units = probe_ref.shape[0] // blocks
    place, outer_at = where_ref[0], where_ref[1]
    own = lax.broadcasted_iota(jnp.int32, (count * rows, lane), 0) % joint
    for u in range(units):
        tiles = [
            tiles_ref[(outer_at ^ b) * inner + (place ^ a), u * unit : (u + 1) * unit, :].astype(f32)
            for a in range(inner)
            for b in away
        ]
        parts = []
        for g in range(groups):
            tile = jnp.concatenate([t[g * rows : (g + 1) * rows] for t in tiles], axis=0)
            spread = jnp.concatenate([jnp.where(own == j, tile, 0.0).astype(bf16) for j in range(joint)], axis=1)
            first = u * blocks + g * joint
            probe = probe_ref[first : first + joint].reshape(joint * lane, width)
            parts.append(jnp.dot(spread, probe, preferred_element_type=f32))
        for a in range(inner):
            for b in range(len(away)):
                at = (a * len(away) + b) * rows
                value = jnp.concatenate([part[at : at + rows] for part in parts], axis=0)
                out_refs[a][b, u * unit : (u + 1) * unit, :] = value.astype(bf16)


def product(where, tiles, probe, inner, bound, away):
    n_dp, slots, _ = tiles.shape
    per_dev, _, width = probe.shape
    joint = joint_of(per_dev)
    groups = 1 if bound * joint % 16 == 0 else 2
    return pl.pallas_call(
        functools.partial(product_kernel, bound, joint, groups, away),
        out_shape=[jax.ShapeDtypeStruct((len(away), slots, width), bf16)] * inner,
        in_specs=[pl.BlockSpec(memory_space=pltpu.SMEM), whole(), whole()],
        out_specs=[whole()] * inner,
        compiler_params=params(),
        cost_estimate=large,
        name="product",
    )(where, tiles, probe)


def choose_kernel(k_j, slots, inner, place_ref, *refs):
    position_refs, out_ref = refs[:-1], refs[-1]
    _, s_dev, count = out_ref.shape
    place, outer_at = place_ref[0], place_ref[1]
    at = lax.broadcasted_iota(jnp.int32, (1, count), 1)
    expect = jnp.zeros((1, count), jnp.int32)
    for a in range(inner):
        inside = jnp.logical_and(at >= a * slots, at < (a + 1) * slots)
        expect = jnp.where(inside, (outer_at * inner + (place ^ a)) * slots + at - a * slots, expect)
    expect = expect.astype(f32)
    rows = [ref[...] for ref in position_refs]
    rows = jnp.concatenate(rows + [jnp.zeros((lane - 8 * len(rows), s_dev), f32)], axis=0)
    columns = jnp.transpose(rows)
    for c in range(len(position_refs)):
        hit = columns[:, 8 * c : 8 * c + 1] == expect
        for k in range(1, k_j):
            hit = jnp.logical_or(hit, columns[:, 8 * c + k : 8 * c + k + 1] == expect)
        out_ref[c] = jnp.where(hit, 1.0, 0.0).astype(bf16)


def choose(where, positions, k_j, slots, inner):
    s_dev = positions[0].shape[1]
    return pl.pallas_call(
        functools.partial(choose_kernel, k_j, slots, inner),
        out_shape=jax.ShapeDtypeStruct((len(positions), s_dev, inner * slots), bf16),
        in_specs=[pl.BlockSpec(memory_space=pltpu.SMEM)] + [whole()] * len(positions),
        out_specs=whole(),
        compiler_params=params(),
        cost_estimate=large,
        name="choose",
    )(where, *positions)


def gather_kernel(away, feat_ref, hits_ref, *refs):
    rows_refs, (keep_ref, give_ref) = refs[:-2], refs[-2:]
    half = hits_ref.shape[1] // 2
    keep_at = pl.multiple_of(feat_ref[0] * half, half)
    give_at = pl.multiple_of((1 - feat_ref[0]) * half, half)
    for at, c in enumerate(away):
        rows = jnp.concatenate([ref[at] for ref in rows_refs], axis=0)
        give_ref[at] = jnp.dot(hits_ref[c, pl.ds(give_at, half), :], rows, preferred_element_type=f32).astype(bf16)
        keep_ref[at] = jnp.dot(hits_ref[c, pl.ds(keep_at, half), :], rows, preferred_element_type=f32)


def gather(feat, hits, rows, away):
    shape = (len(away), hits.shape[1] // 2, rows[0].shape[2])
    return pl.pallas_call(
        functools.partial(gather_kernel, away),
        out_shape=(jax.ShapeDtypeStruct(shape, f32), jax.ShapeDtypeStruct(shape, bf16)),
        in_specs=[pl.BlockSpec(memory_space=pltpu.SMEM)] + [whole()] * (1 + len(rows)),
        out_specs=(whole(), whole()),
        compiler_params=params(),
        cost_estimate=large,
        name="gather",
    )(feat.reshape(1), hits, *rows)


def combine_kernel(k_j, position_ref, rows_ref, out_ref):
    step = pl.program_id(0)
    s_dev = position_ref.shape[1]
    count = rows_ref.shape[0]
    here = lax.broadcasted_iota(jnp.int32, (s_dev, count), 1) + step * count
    rows = jnp.concatenate([position_ref[...], jnp.zeros((lane - 8, s_dev), f32)], axis=0)
    position = jnp.transpose(rows).astype(jnp.int32)
    hit = position[:, 0:1] == here
    for k in range(1, k_j):
        hit = jnp.logical_or(hit, position[:, k : k + 1] == here)
    part = jnp.dot(jnp.where(hit, 1.0, 0.0).astype(bf16), rows_ref[...], preferred_element_type=f32)

    @pl.when(step == 0)
    def _():
        out_ref[...] = part

    @pl.when(step > 0)
    def _():
        out_ref[...] += part


def combine(position, rows, k_j):
    s_dev = position.shape[1]
    total, width = rows.shape
    count = total // 6 if total % (6 * lane) == 0 else total
    return pl.pallas_call(
        functools.partial(combine_kernel, k_j),
        out_shape=jax.ShapeDtypeStruct((s_dev, width), f32),
        grid=(total // count,),
        in_specs=[
            pl.BlockSpec((8, s_dev), lambda i: (0, 0)),
            pl.BlockSpec((count, width), lambda i: (i, 0)),
        ],
        out_specs=pl.BlockSpec((s_dev, width), lambda i: (0, 0)),
        compiler_params=params(),
        name="combine",
    )(position, rows)


def block_pairs(width):
    n = width // lane
    return [(i, j) for i in range(n) for j in range(i, n)]


def gram_kernel(pairs_ref, sketch_ref, gram_ref):
    for at in range(gram_ref.shape[0]):
        left = sketch_ref[:, pl.ds(pl.multiple_of(pairs_ref[2 * at] * lane, lane), lane)]
        right = sketch_ref[:, pl.ds(pl.multiple_of(pairs_ref[2 * at + 1] * lane, lane), lane)]
        gram_ref[at] = lax.dot_general(left, right, COLS, preferred_element_type=f32).astype(bf16)


def gram_blocks(sketch, feat):
    width = sketch.shape[1]
    pairs = block_pairs(width)
    half = len(pairs) // 2
    table = jnp.asarray(np.array(pairs, np.int32).reshape(2, 2 * half))
    smem = pl.BlockSpec(memory_space=pltpu.SMEM)
    return pl.pallas_call(
        gram_kernel,
        out_shape=jax.ShapeDtypeStruct((half, lane, lane), bf16),
        in_specs=[smem, whole()],
        out_specs=whole(),
        compiler_params=params(),
        name="gram",
    )(table[feat % 2], sketch)


def halves(value):
    high = value.astype(bf16)
    return high, (value - high.astype(f32)).astype(bf16)


def dot(a, b):
    return jnp.dot(a, b, preferred_element_type=f32)


def dot3(a, b):
    (ah, al), (bh, bl) = halves(a), halves(b)
    return dot(jnp.concatenate([al, ah, ah], axis=1), jnp.concatenate([bh, bl, bh], axis=0))


def root_kernel(samples, place_ref, mine_gram_ref, other_gram_ref, mine_ref, out_ref, gram):
    width = mine_ref.shape[1]
    pairs = block_pairs(width)
    half = len(pairs) // 2
    odd = place_ref[0] % 2 == 1
    for at, (i, j) in enumerate(pairs):
        mine, other = mine_gram_ref[at % half].astype(f32), other_gram_ref[at % half].astype(f32)
        block = jnp.where(odd == (at < half), other, mine)
        gram[i * lane : (i + 1) * lane, j * lane : (j + 1) * lane] = block
        if i != j:
            gram[j * lane : (j + 1) * lane, i * lane : (i + 1) * lane] = jnp.transpose(block)
    rows = lax.broadcasted_iota(jnp.int32, (width, width), 0)
    ident = jnp.where(rows == lax.broadcasted_iota(jnp.int32, (width, width), 1), 1.0, 0.0)
    total = gram[...] + ridge * samples * ident
    scale = jnp.sum(total * ident, axis=(0, 1), keepdims=True) / width
    gap = 0.5 * ident - 0.5 * (total / scale)
    high, low = halves(gap)
    mine = mine_ref[...]
    value = mine.astype(f32) + dot(jnp.concatenate([mine, mine], axis=1), jnp.concatenate([low, high], axis=0))
    square = dot3(gap, gap)
    part, rest = halves(square)
    gap = 1.5 * square + dot(jnp.concatenate([rest, part], axis=1), jnp.concatenate([high, high], axis=0))
    for _ in range(root_steps - 3):
        high = gap.astype(bf16)
        value = value + dot(value.astype(bf16), high)
        square = dot(high, high)
        gap = 1.5 * square + dot(square.astype(bf16), high)
    high = gap.astype(bf16)
    value = value + dot(value.astype(bf16), high)
    moved = dot(dot(value.astype(bf16), high).astype(bf16), high)
    value = value + 1.5 * moved + dot(moved.astype(bf16), high)
    out_ref[...] = (math.sqrt(samples) * lax.rsqrt(scale)) * value


def whiten(mine_gram, other_gram, mine, place, samples):
    width = mine.shape[1]
    return pl.pallas_call(
        functools.partial(root_kernel, samples),
        out_shape=jax.ShapeDtypeStruct(mine.shape, f32),
        in_specs=[pl.BlockSpec(memory_space=pltpu.SMEM), whole(), whole(), whole()],
        out_specs=whole(),
        scratch_shapes=[pltpu.VMEM((width, width), f32)],
        compiler_params=params(),
        name="root",
    )(place.reshape(1), mine_gram, other_gram, mine)


def crossed(value, axis, bits):
    count = lax.axis_size(axis)
    return lax.ppermute(value, axis, [(source, source ^ bits) for source in range(count)])


def total_of(values):
    total = values[0].astype(f32)
    for value in values[1:]:
        total = total + value.astype(f32)
    return total


def sum_over_dp(value):
    n_dp = lax.axis_size("dp")
    inner = math.gcd(n_dp, 4)
    me = lax.axis_index("dp") & (inner - 1)
    flat = value.reshape(-1, lane)
    rows = flat.shape[0] // inner
    parts = [lax.dynamic_slice_in_dim(flat, (me ^ bits) * rows, rows, 0) for bits in range(inner)]
    part = total_of([parts[0]] + [crossed(parts[bits], "dp", bits) for bits in range(1, inner)]).astype(bf16)
    if n_dp // inner == 4:
        part = total_of([part] + [crossed(part, "dp", bits * inner) for bits in range(1, 4)]).astype(bf16)
    else:
        bits = inner
        while bits < n_dp:
            part = total_of([part, crossed(part, "dp", bits)]).astype(bf16)
            bits *= 2
    pieces = jnp.stack([part] + [crossed(part, "dp", bits) for bits in range(1, inner)])
    return jnp.concatenate([pieces[me ^ at] for at in range(inner)], axis=0).reshape(value.shape)


def sketch_by_all_to_all(products, position, k_j):
    n_feat = lax.axis_size("feat")
    feat = lax.axis_index("feat")
    width = products.shape[2]
    returned = lax.all_to_all(products, "dp", split_axis=0, concat_axis=0, tiled=True)
    part = combine(position, returned.reshape(-1, width), k_j)
    bits = 1
    while bits < n_feat:
        part = part + crossed(part, "feat", bits)
        bits *= 2
    sketch = part.astype(bf16)
    own_rows = sketch.shape[0] // n_feat
    return lax.dynamic_slice_in_dim(sketch, feat * own_rows, own_rows, 0), sketch


def tied(value, *others):
    return lax.optimization_barrier((value, others))[0]


def sketch_by_planes(tiles, probe, position, inner, bound, k_j):
    n_dp, slots, _ = tiles.shape
    index, feat = lax.axis_index("dp"), lax.axis_index("feat")
    where = jnp.stack([index & (inner - 1), index // inner])
    positions = [position] + [crossed(position, "dp", c * inner) for c in range(1, n_dp // inner)]
    sent, hits = [], None
    for at, away in enumerate(stages[:3]):
        behind = positions if not at else sent[-1]
        if at == 2:
            hits = choose(where, tied(positions, sent[-1]), k_j, slots, inner)
            behind = hits
        sent.append(product(where, tied(tiles, behind), probe, inner, bound, away))
    plane, kept, behind = {}, [], None
    for at, away in enumerate(stages):
        if at == 1:
            sent.append(product(where, tied(tiles, kept[0]), probe, inner, bound, stages[3]))
        rows = [sent[at][0]] + [crossed(sent[at][a], "dp", a) for a in range(1, inner)]
        if at:
            rows = tied(rows, kept[-1], (plane[3], sent[3]) if at == 2 else (plane[2], plane[1]) if at == 3 else sent[3])
        keep, give = gather(feat, hits, rows, away)
        kept.append(keep)
        both = keep + crossed(give, "feat", 1).astype(f32)
        plane.update({c: both[i] for i, c in enumerate(away)})
        if at == 1:
            plane[2] = plane[2] + crossed(plane[3].astype(bf16), "dp", inner).astype(f32)
    plane[0] = plane[0] + crossed(plane[1].astype(bf16), "dp", inner).astype(f32)
    mine = (plane[0] + crossed(plane[2].astype(bf16), "dp", 2 * inner).astype(f32)).astype(bf16)
    return mine, jnp.concatenate([mine, crossed(mine, "feat", 1)], axis=0)


def local(grads, block_ids, probe):
    values = grads[0]
    s_dev, k_j, b_width = values.shape
    n_dp, n_feat = lax.axis_size("dp"), lax.axis_size("feat")
    feat = lax.axis_index("feat")
    per_dev = probe.shape[0]
    width = probe.shape[3]
    b_slice = per_dev * n_dp
    bound = max(2, 3 * s_dev * k_j // (2 * b_slice))
    probe = probe[:, 0]
    send, position = pack(block_ids[0].T, values.reshape(s_dev * k_j, b_width), n_dp, per_dev, bound)
    tiles = lax.all_to_all(send, "dp", split_axis=0, concat_axis=0, tiled=True)
    if n_feat == 2 and n_dp == 16:
        mine, sketch = sketch_by_planes(tiles, probe, position, 4, bound, k_j)
    else:
        products = product(jnp.zeros((2,), jnp.int32), tiles, probe, 1, bound, tuple(range(n_dp)))
        mine, sketch = sketch_by_all_to_all(products[0], position, k_j)
    mine_gram = sum_over_dp(gram_blocks(sketch, feat))
    other_gram = crossed(mine_gram, "feat", 1)
    return whiten(mine_gram, other_gram, mine, feat, s_dev * n_dp)


def solution(mesh):
    return jax.shard_map(
        local,
        mesh=mesh,
        in_specs=(P("feat", "dp", None, None), P("feat", "dp", None), P("dp", "feat", None, None)),
        out_specs=P(("dp", "feat"), None),
        check_vma=False,
    )
```
